512 devices in a mesh: seq: 64 (over y, x, core), head: 8 (over z).
Axes of the slice: x: 4, y: 8, z: 8, core: 2. Of those that a mesh axis runs over, the one named last changes fastest.
Arguments:
- activations: bfloat16 [16384, 4096], P('seq', 'head'), may hold values from -6 to 6
- grad_out: bfloat16 [16384, 4096], P('seq', 'head'), may hold values from -0.03125 to 0.03125
- query_weight: bfloat16 [4096, 4096], P('seq', 'head'), may hold values from -0.09375 to 0.09375
- key_weight: bfloat16 [4096, 1024], P('seq', 'head'), may hold values from -0.09375 to 0.09375
- value_weight: bfloat16 [4096, 1024], P('seq', 'head'), may hold values from -0.09375 to 0.09375
Outputs:
- grad_input: bfloat16 [16384, 4096], P('seq', 'head')
The draws below stay inside these ranges and needn't reach their ends.
All inputs are finite; a program needn't handle non-finite values.
Results may differ from the reference program's by a relative error of at most 0.018.
Values may be sent and summed in bfloat16 or wider, within the bound.
A program may use at most 64 MiB of HBM per device.

```python
import jax
import jax.numpy as jnp
from jax import lax

D = 4096
HEADS = 32
KV_HEADS = 8
HEAD_DIM = 128
TOK_DEV = 256
TOKENS = 16384


def shard_levels(rng, dims, shards, low, top_value):
    gain, own = 1.0, jax.random.fold_in(rng, 6)
    for axis_at, shards_of in shards:
        heights = jnp.exp(jax.random.uniform(jax.random.fold_in(own, axis_at), (shards_of,), jnp.float32, low / len(shards), top_value / len(shards)))
        gain = gain * jnp.repeat(heights, dims[axis_at] // shards_of).reshape([-1 if axis == axis_at else 1 for axis in range(len(dims))])
    return gain


def noise(stream_key, shape, width, most, pieces=(), dtype=jnp.bfloat16):
    array = width * jax.random.normal(stream_key, shape, jnp.float32)
    if pieces:
        array = array * shard_levels(stream_key, shape, pieces, -0.22, 0.18)
    return jnp.clip(array, -most, most).astype(dtype)


def setup_inputs(seed: int = 0) -> dict:
    key_list = jax.random.split(jax.random.key(seed), 6)
    activations = noise(key_list[0], (TOKENS, D), 1.0, 6.0, ((0, 64), (1, 8)))
    grad_out = noise(key_list[1], (TOKENS, HEADS * HEAD_DIM), 0.005, 0.03125, ((0, 64), (1, 8)))
    query_weight = noise(key_list[2], (D, HEADS * HEAD_DIM), D ** -0.5, 0.09375, ((0, 64), (1, 8)))
    key_weight = noise(key_list[3], (D, KV_HEADS * HEAD_DIM), D ** -0.5, 0.09375, ((0, 64), (1, 8)))
    value_weight = noise(key_list[4], (D, KV_HEADS * HEAD_DIM), D ** -0.5, 0.09375, ((0, 64), (1, 8)))
    return dict(activations=activations, grad_out=grad_out, query_weight=query_weight, key_weight=key_weight, value_weight=value_weight)


def reference(activations, grad_out, query_weight, key_weight, value_weight):
    factor = HEAD_DIM ** -0.5
    group_size = HEADS // KV_HEADS
    shard_count = TOKENS // TOK_DEV
    queries = jnp.dot(activations, query_weight, preferred_element_type=jnp.float32).astype(jnp.bfloat16)
    key_rows = jnp.dot(activations, key_weight, preferred_element_type=jnp.float32).astype(jnp.bfloat16)
    value_rows = jnp.dot(activations, value_weight, preferred_element_type=jnp.float32).astype(jnp.bfloat16)
    queries, key_rows, value_rows = lax.optimization_barrier((queries, key_rows, value_rows))
    query_heads = queries.reshape(shard_count, TOK_DEV, KV_HEADS, group_size, HEAD_DIM)
    key_heads = key_rows.reshape(shard_count, TOK_DEV, KV_HEADS, HEAD_DIM)
    value_heads = value_rows.reshape(shard_count, TOK_DEV, KV_HEADS, HEAD_DIM)
    grad_heads = grad_out.reshape(shard_count, TOK_DEV, KV_HEADS, group_size, HEAD_DIM)
    kv_state = jnp.einsum('ntgd,ntge->ngde', key_heads.astype(jnp.float32), value_heads.astype(jnp.float32)).astype(jnp.bfloat16)
    grad_state = (factor * jnp.einsum('ntghd,ntghe->ngde', query_heads.astype(jnp.float32), grad_heads.astype(jnp.float32))).astype(jnp.bfloat16)
    kv_state, grad_state = lax.optimization_barrier((kv_state, grad_state))
    kv_wide = kv_state.astype(jnp.float32)
    grad_wide = grad_state.astype(jnp.float32)
    running = jnp.cumsum(kv_wide, axis=0)
    prefix = jnp.concatenate([jnp.zeros_like(running[:1]), running[:-1]], axis=0)
    behind = jnp.cumsum(grad_wide[::-1], axis=0)[::-1]
    suffix = jnp.concatenate([behind[1:], jnp.zeros_like(behind[:1])], axis=0)
    prefix_half, suffix_half = lax.optimization_barrier((prefix.astype(jnp.bfloat16), suffix.astype(jnp.bfloat16)))
    causal = jnp.arange(TOK_DEV)[:, None] >= jnp.arange(TOK_DEV)[None, :]

    def one_shard(items):
        query_blk, key_blk, value_blk, grad_blk, prefix_blk, suffix_blk = items
        query_wide = query_blk.astype(jnp.float32)
        key_wide = key_blk.astype(jnp.float32)
        value_wide = value_blk.astype(jnp.float32)
        grad_wide_blk = grad_blk.astype(jnp.float32)
        prefix_wide = prefix_blk.astype(jnp.float32)
        suffix_wide = suffix_blk.astype(jnp.float32)
        scores = jnp.where(causal, jnp.einsum('tghd,sgd->ghts', query_wide, key_wide), 0.0).astype(jnp.bfloat16)
        grad_scores = jnp.where(causal, jnp.einsum('tghe,sge->ghts', grad_wide_blk, value_wide), 0.0).astype(jnp.bfloat16)
        scores, grad_scores = lax.optimization_barrier((scores, grad_scores))
        scores_wide = scores.astype(jnp.float32)
        grad_scores_wide = grad_scores.astype(jnp.float32)
        grad_query = factor * (jnp.einsum('ghts,sgd->tghd', grad_scores_wide, key_wide) + jnp.einsum('tghe,gde->tghd', grad_wide_blk, prefix_wide))
        grad_key = factor * jnp.einsum('ghts,tghd->sgd', grad_scores_wide, query_wide) + jnp.einsum('sge,gde->sgd', value_wide, suffix_wide)
        grad_value = factor * jnp.einsum('ghts,tghe->sge', scores_wide, grad_wide_blk) + jnp.einsum('sgd,gde->sge', key_wide, suffix_wide)
        return (grad_query.astype(jnp.bfloat16).reshape(TOK_DEV, -1),
                grad_key.astype(jnp.bfloat16).reshape(TOK_DEV, -1),
                grad_value.astype(jnp.bfloat16).reshape(TOK_DEV, -1))

    grad_query, grad_key, grad_value = lax.map(one_shard, (query_heads, key_heads, value_heads, grad_heads, prefix_half, suffix_half))
    grad_query = grad_query.reshape(TOKENS, -1)
    grad_key = grad_key.reshape(TOKENS, -1)
    grad_value = grad_value.reshape(TOKENS, -1)
    total = jnp.dot(grad_query, query_weight.T, preferred_element_type=jnp.float32)
    total = total + jnp.dot(grad_key, key_weight.T, preferred_element_type=jnp.float32)
    total = total + jnp.dot(grad_value, value_weight.T, preferred_element_type=jnp.float32)
    return total.astype(jnp.bfloat16)
```

```python
import jax
import jax.numpy as jnp
from jax import lax
from jax.experimental import pallas as pl
from jax.experimental.pallas import tpu as pltpu
from jax.sharding import Mesh
from jax.sharding import PartitionSpec as P

HEADS = 32
KV_HEADS = 8
HD = 128
GROUP = HEADS // KV_HEADS
NY, NX, NC, NZ = 8, 4, 2, 8
ROW = NX * NC
AXES = ("y", "x", "core", "head")
SEQ = ("y", "x", "core")
F32 = jnp.float32
BF16 = jnp.bfloat16
TOK = 256
FEAT = 512
WROWS = 64
WCOLS = 768
SUBS = 4
SUB = TOK // SUBS
HALF = NZ // 2
R_ORDER = (0, 1, 2, 3)
L_ORDER = (2, 3, 0, 1)
R_LAST = (0, 1)
L_LAST = (2, 3)
X_ORDER = (0, 1, 3, 2)
XR_LAST = (0, 1)
XL_LAST = (3, 2)


def nt(a, b):
    return lax.dot_general(a, b, (((1,), (1,)), ((), ())), preferred_element_type=F32)


def tn(a, b):
    return lax.dot_general(a, b, (((0,), (0,)), ((), ())), preferred_element_type=F32)


def nn(a, b):
    return jnp.dot(a, b, preferred_element_type=F32)


def kernel(
    a_ref, g_ref, wq_ref, wk_ref, wv_ref, o_ref,
    act, wts, acc, qkv, dq, dk, dv, grads, part, tx, rx,
    st, in1, tot, in2, out3, in3,
    z_send, z_recv, w_send, w_recv, s_send, s_recv, e_send, e_recv, r_send, r_recv,
):
    y, x, c, z = (lax.axis_index(n) for n in AXES)
    r = x * NC + c
    n_y = lambda d: lax.rem(y + d + NY, NY)
    n_x = lambda d: lax.rem(x + d + NX, NX)
    n_z = lambda d: lax.rem(z + d + NZ, NZ)
    n_r = lambda d: lax.rem(r + d + ROW, ROW)
    zr, zl = {"head": n_z(1)}, {"head": n_z(-1)}
    yr, yl = {"y": n_y(1)}, {"y": n_y(-1)}
    xr, xl = {"x": n_x(1)}, {"x": n_x(-1)}
    sib = {"core": 1 - c}
    row_peer = lambda d: {"x": n_r(d) // NC, "core": lax.rem(n_r(d), NC)}

    barrier = pltpu.get_barrier_semaphore()
    peers = [zr, zl] + [row_peer(d) for d in range(1, ROW)] + [{"y": n_y(d)} for d in range(1, NY)]
    for peer in peers:
        pl.semaphore_signal(barrier, inc=1, device_id=peer, device_id_type=pl.DeviceIdType.MESH)

    act[z] = a_ref[...]
    wts[y, x, c, :, 0:512] = wq_ref[...]
    wts[y, x, c, :, 512:640] = wk_ref[...]
    wts[y, x, c, :, 640:768] = wv_ref[...]
    pl.semaphore_wait(barrier, len(peers))

    def copy(src, dst, ssem, rsem, dev):
        return pltpu.make_async_remote_copy(
            src_ref=src, dst_ref=dst, send_sem=ssem, recv_sem=rsem,
            device_id=dev, device_id_type=pl.DeviceIdType.MESH,
        )

    def same(ref, ssem, rsem, dev):
        return copy(ref, ref, ssem, rsem, dev)

    def z_msg(d, k, s):
        origin = n_z(1 - k) if d == 0 else n_z(k - 1)
        ref = act.at[origin, pl.ds(s * SUB, SUB)]
        return same(ref, z_send.at[d, k, s], z_recv.at[d, k, s], zr if d == 0 else zl)

    def z_wait(d, k, s):
        origin = n_z(-k) if d == 0 else n_z(k)
        ref = act.at[origin, pl.ds(s * SUB, SUB)]
        same(ref, z_send.at[d, k, s], z_recv.at[d, k, s], zr if d == 0 else zl).wait_recv()

    def z_has(d, k, s):
        return k < HALF or (k == HALF and s in (R_LAST if d == 0 else L_LAST))

    def z_start():
        for i in range(SUBS):
            z_msg(0, 1, R_ORDER[i]).start()
            z_msg(1, 1, L_ORDER[i]).start()

    z_ticks = []
    for k in range(1, HALF + 1):
        for i in range(SUBS):
            pair = [(0, k, R_ORDER[i]), (1, k, L_ORDER[i])]
            pair = [p for p in pair if z_has(*p)]
            if pair:
                z_ticks.append(pair)

    def z_tick(i):
        for d, k, s in z_ticks[i]:
            z_wait(d, k, s)
            if z_has(d, k + 1, s):
                z_msg(d, k + 1, s).start()

    def w_ref(dy, dx, core, half=None):
        ref = wts.at[n_y(dy), n_x(dx), core]
        return ref if half is None else ref.at[pl.ds(32 * half, 32)]

    def w_msg(ref, i, dev):
        return same(ref, w_send.at[i], w_recv.at[i], dev)

    def sib_msg(m, core):
        ref = wts.at[n_y(m), :, core]
        return same(ref, s_send.at[m % NY], s_recv.at[m % NY], sib)

    def core0():
        slot = lambda d, k, j: 4 + (d * 5 + k) * 4 + j

        def has(d, k, j):
            return k < 4 or (k == 4 and j in (XR_LAST if d == 0 else XL_LAST))

        def y_msg(d, k, j):
            dy = (1 - k) if d == 0 else (k - 1)
            return w_msg(w_ref(dy, j, 0), slot(d, k, j), yr if d == 0 else yl)

        def y_wait(d, k, j):
            dy = -k if d == 0 else k
            w_msg(w_ref(dy, j, 0), slot(d, k, j), yr if d == 0 else yl).wait_recv()

        def y_both(j):
            y_msg(0, 1, j).start()
            y_msg(1, 1, j).start()

        w_msg(w_ref(0, 0, 0), 0, xr).start()
        w_msg(w_ref(0, 0, 0), 1, xl).start()
        y_both(0)
        z_start()
        w_msg(w_ref(0, 1, 0), 1, xl).wait_recv()
        w_msg(w_ref(0, 1, 0, 1), 3, xl).start()
        y_both(1)
        w_msg(w_ref(0, -1, 0), 0, xr).wait_recv()
        w_msg(w_ref(0, -1, 0, 0), 2, xr).start()
        y_both(3)
        z_tick(0)
        w_msg(w_ref(0, -2, 0, 0), 2, xr).wait_recv()
        w_msg(w_ref(0, 2, 0, 1), 3, xl).wait_recv()
        y_both(2)
        sib_msg(0, 0).start()

        events = []
        for k in range(1, 5):
            for j in X_ORDER:
                todo = [d for d in (0, 1) if has(d, k, j)]
                events.append((k, j, todo))
        merged = [[e] for e in events[:12]]
        merged.append([events[12], events[14]])
        merged.append([events[13], events[15]])
        for i in range(14):
            if i > 0:
                z_tick(i)
            for k, j, todo in merged[i]:
                for d in todo:
                    y_wait(d, k, j)
                    if has(d, k + 1, j):
                        y_msg(d, k + 1, j).start()
            if i in (3, 7, 11):
                k = (i + 1) // 4
                sib_msg(-k, 0).start()
                sib_msg(k, 0).start()
        sib_msg(4, 0).start()

        for i in range(4):
            dx, half, dev = ((0, None, xr), (0, None, xl), (-1, 0, xr), (1, 1, xl))[i]
            w_msg(w_ref(0, dx, 0, half), i, dev).wait_send()
        for k in range(1, 5):
            for j in range(4):
                for d in (0, 1):
                    if has(d, k, j):
                        y_msg(d, k, j).wait_send()

    def core1():
        def y_msg(d, k):
            dy = (1 - k) if d == 0 else (k - 1)
            half = None if k < 4 else d
            return w_msg(w_ref(dy, 0, 1, half), d * 5 + k, yr if d == 0 else yl)

        def y_wait(d, k):
            dy = -k if d == 0 else k
            half = None if k < 4 else d
            w_msg(w_ref(dy, 0, 1, half), d * 5 + k, yr if d == 0 else yl).wait_recv()

        def x_first(m):
            i = 10 + (m % NY) * 4
            return [w_msg(w_ref(m, 0, 1), i, xr), w_msg(w_ref(m, 0, 1), i + 1, xl)]

        def x_second(m, d):
            i = 10 + (m % NY) * 4
            return w_msg(w_ref(m, 2 * d - 1, 1, d), i + 2 + d, xl if d else xr)

        def x_send(m):
            for msg in x_first(m):
                msg.start()

        def x_mid(m):
            i = 10 + (m % NY) * 4
            w_msg(w_ref(m, -1, 1), i, xr).wait_recv()
            x_second(m, 0).start()
            w_msg(w_ref(m, 1, 1), i + 1, xl).wait_recv()
            x_second(m, 1).start()

        def x_end(m):
            i = 10 + (m % NY) * 4
            w_msg(w_ref(m, -2, 1, 0), i + 2, xr).wait_recv()
            w_msg(w_ref(m, 2, 1, 1), i + 3, xl).wait_recv()
            sib_msg(m, 1).start()

        def y_event(k):
            for d in (0, 1):
                y_wait(d, k)
                if k < 4:
                    y_msg(d, k + 1).start()
                    x_send(-k if d == 0 else k)
            if k == 4:
                x_send(4)

        y_msg(0, 1).start()
        y_msg(1, 1).start()
        x_send(0)
        z_start()
        plan = [
            lambda: x_mid(0), lambda: y_event(1), lambda: x_end(0), lambda: (x_mid(-1), x_mid(1)),
            lambda: y_event(2), lambda: (x_end(-1), x_end(1)), lambda: (x_mid(-2), x_mid(2)),
            lambda: y_event(3), lambda: (x_end(-2), x_end(2)), lambda: (x_mid(-3), x_mid(3)),
            lambda: y_event(4), lambda: (x_end(-3), x_end(3)), lambda: x_mid(4), lambda: x_end(4),
        ]
        for i in range(14):
            plan[i]()
            z_tick(i)
        for d in (0, 1):
            for k in range(1, 5):
                y_msg(d, k).wait_send()
        for m in range(NY):
            for msg in x_first(m) + [x_second(m, 0), x_second(m, 1)]:
                msg.wait_send()

    pl.when(c == 0)(core0)
    pl.when(c == 1)(core1)

    for m in range(NY):
        ref = wts.at[n_y(m), :, 1 - c]
        same(ref, s_send.at[m], s_recv.at[m], sib).wait_recv()
    for m in range(NY):
        sib_msg(m, c).wait_send()
    for pair in [(d, k, s) for d in (0, 1) for k in range(1, HALF + 1) for s in range(SUBS)]:
        if z_has(*pair):
            z_msg(*pair).wait_send()

    acc[...] = jnp.zeros_like(acc)

    @pl.loop(0, NZ)
    def _(f):
        acc[...] += nn(act[f], wts[f].reshape(FEAT, WCOLS))

    qkv[...] = acc[...].astype(BF16)
    head = lambda h: pl.ds(h * HD, HD)
    k_val, v_val = qkv[:, 512:640], qkv[:, 640:768]
    factor = HD ** -0.5
    kv = tn(k_val, v_val)
    gs = tn(qkv[:, head(0)], g_ref[:, head(0)])
    for h in range(1, GROUP):
        gs += tn(qkv[:, head(h)], g_ref[:, head(h)])
    st[:, 0] = kv.astype(BF16).reshape(ROW, HD // ROW, HD)
    st[:, 1] = (factor * gs).astype(BF16).reshape(ROW, HD // ROW, HD)

    def e1(d):
        return copy(st.at[n_r(d)], in1.at[r], e_send.at[0, d], e_recv.at[0, d], row_peer(d))

    def e1_wait(d):
        copy(st.at[r], in1.at[n_r(-d)], e_send.at[0, d], e_recv.at[0, d], row_peer(d)).wait_recv()

    for d in range(1, ROW):
        e1(d).start()
    in1[r] = st[r]
    rows_t = lax.broadcasted_iota(jnp.int32, (TOK, TOK), 0)
    cols_s = lax.broadcasted_iota(jnp.int32, (TOK, TOK), 1)
    causal = rows_t >= cols_s

    def attend(h):
        q_h, g_h = qkv[:, head(h)], g_ref[:, head(h)]
        k_v, v_v = qkv[:, 512:640], qkv[:, 640:768]
        s = jnp.where(causal, nt(q_h, k_v), 0.0).astype(BF16)
        gsc = jnp.where(causal, nt(g_h, v_v), 0.0).astype(BF16)
        dq[:, head(h)] = nn(gsc, k_v)
        if h == 0:
            dk[...] = tn(gsc, q_h)
            dv[...] = tn(s, g_h)
        else:
            dk[...] += tn(gsc, q_h)
            dv[...] += tn(s, g_h)

    attend(0)
    for d in range(1, ROW):
        e1_wait(d)
    pieces = [in1[i].astype(F32) for i in range(ROW)]
    total = pieces[0]
    for i in range(1, ROW):
        total = total + pieces[i]
    tot[...] = total.astype(BF16)

    def e2(d):
        return copy(tot, in2.at[y], e_send.at[1, d], e_recv.at[1, d], {"y": n_y(d)})

    def e2_wait(d):
        copy(tot, in2.at[n_y(-d)], e_send.at[1, d], e_recv.at[1, d], {"y": n_y(d)}).wait_recv()

    for d in range(1, NY):
        e2(d).start()
    in2[y] = tot[...]
    attend(1)
    attend(2)
    for d in range(1, NY):
        e2_wait(d)
    before = jnp.zeros((HD // ROW, HD), F32)
    after = jnp.zeros((HD // ROW, HD), F32)
    for i in range(NY):
        one = in2[i].astype(F32)
        before = before + jnp.where(i < y, one[0], 0.0)
        after = after + jnp.where(i > y, one[1], 0.0)
    for i in range(ROW):
        out3[i, 0] = before.astype(BF16)
        before = before + pieces[i][0]
    for i in reversed(range(ROW)):
        out3[i, 1] = after.astype(BF16)
        after = after + pieces[i][1]

    def e3(d):
        return copy(out3.at[n_r(d)], in3.at[r], e_send.at[2, d], e_recv.at[2, d], row_peer(d))

    def e3_wait(d):
        copy(out3.at[r], in3.at[n_r(-d)], e_send.at[2, d], e_recv.at[2, d], row_peer(d)).wait_recv()

    for d in range(1, ROW):
        e3(d).start()
    in3[r] = out3[r]
    attend(3)
    for d in range(1, ROW):
        e3_wait(d)
    for d in range(1, ROW):
        e1(d).wait_send()
        e2(d).wait_send()
        e3(d).wait_send()
    prefix = in3[:, 0].reshape(HD, HD)
    suffix = in3[:, 1].reshape(HD, HD)
    for h in range(GROUP):
        cross = nt(g_ref[:, head(h)], prefix)
        grads[:, head(h)] = (factor * (dq[:, head(h)] + cross)).astype(BF16)
    grads[:, 512:640] = (factor * dk[...] + nt(qkv[:, 640:768], suffix)).astype(BF16)
    grads[:, 640:768] = (factor * dv[...] + nn(qkv[:, 512:640], suffix)).astype(BF16)

    def share(dz, slot):
        part[slot] = nt(grads[...], wts[n_z(dz)].reshape(FEAT, WCOLS))

    def r_msg(d, k, s):
        ds = pl.ds(s * SUB, SUB)
        return copy(tx.at[d, k - 1, ds], rx.at[d, k - 1, ds], r_send.at[d, k, s], r_recv.at[d, k, s], zr if d == 0 else zl)

    def r_step(d, k, s):
        ds = pl.ds(s * SUB, SUB)
        value = part[d, ds]
        if z_has(d, k + 1, s):
            r_msg(d, k + 1, s).wait_recv()
            value = value + rx[d, k, ds].astype(F32)
        tx[d, k - 1, ds] = value.astype(BF16)
        r_msg(d, k, s).start()

    share(HALF, 0)
    for d in (0, 1):
        for s in (R_LAST if d == 0 else L_LAST):
            ds = pl.ds(s * SUB, SUB)
            tx[d, HALF - 1, ds] = part[0, ds].astype(BF16)
            r_msg(d, HALF, s).start()
    for k in range(HALF - 1, 0, -1):
        share(k, 0)
        share(-k, 1)
        for i in range(SUBS):
            r_step(0, k, L_ORDER[i])
            r_step(1, k, R_ORDER[i])
    share(0, 0)
    for i in range(SUBS):
        s = L_ORDER[i]
        ds = pl.ds(s * SUB, SUB)
        r_msg(0, 1, s).wait_recv()
        r_msg(1, 1, s).wait_recv()
        o_ref[ds] = (part[0, ds] + rx[0, 0, ds].astype(F32) + rx[1, 0, ds].astype(F32)).astype(BF16)
    for d in (0, 1):
        for k in range(1, HALF + 1):
            for s in range(SUBS):
                if z_has(d, k, s):
                    r_msg(d, k, s).wait_send()


def local(activations, grad_out, query_weight, key_weight, value_weight):
    dma = pltpu.SemaphoreType.DMA
    return pl.pallas_call(
        kernel,
        out_shape=jax.ShapeDtypeStruct((TOK, FEAT), BF16),
        in_specs=[pl.BlockSpec(memory_space=pltpu.VMEM)] * 5,
        out_specs=pl.BlockSpec(memory_space=pltpu.VMEM),
        scratch_shapes=[
            pltpu.VMEM((NZ, TOK, FEAT), BF16),
            pltpu.VMEM((NY, NX, NC, WROWS, WCOLS), BF16),
            pltpu.VMEM((TOK, WCOLS), F32),
            pltpu.VMEM((TOK, WCOLS), BF16),
            pltpu.VMEM((TOK, FEAT), F32),
            pltpu.VMEM((TOK, HD), F32),
            pltpu.VMEM((TOK, HD), F32),
            pltpu.VMEM((TOK, WCOLS), BF16),
            pltpu.VMEM((2, TOK, FEAT), F32),
            pltpu.VMEM((2, HALF, TOK, FEAT), BF16),
            pltpu.VMEM((2, HALF, TOK, FEAT), BF16),
            pltpu.VMEM((ROW, 2, HD // ROW, HD), BF16),
            pltpu.VMEM((ROW, 2, HD // ROW, HD), BF16),
            pltpu.VMEM((2, HD // ROW, HD), BF16),
            pltpu.VMEM((NY, 2, HD // ROW, HD), BF16),
            pltpu.VMEM((ROW, 2, HD // ROW, HD), BF16),
            pltpu.VMEM((ROW, 2, HD // ROW, HD), BF16),
            dma((2, HALF + 1, SUBS)),
            dma((2, HALF + 1, SUBS)),
            dma((44,)),
            dma((44,)),
            dma((NY,)),
            dma((NY,)),
            dma((3, 8)),
            dma((3, 8)),
            dma((2, HALF + 1, SUBS)),
            dma((2, HALF + 1, SUBS)),
        ],
        compiler_params=pltpu.CompilerParams(
            collective_id=0, has_side_effects=True, vmem_limit_bytes=48 * 1024 * 1024
        ),
        cost_estimate=pl.CostEstimate(flops=4_000_000_000, bytes_accessed=2_000_000, transcendentals=0),
    )(activations, grad_out, query_weight, key_weight, value_weight)


def solution(mesh):
    finer = Mesh(mesh.devices.reshape(NY, NX, NC, NZ), AXES)
    spec = P(SEQ, "head")
    return jax.shard_map(
        local, mesh=finer, in_specs=(spec,) * 5, out_specs=spec, check_vma=False
    )
```

```python
import jax
import jax.numpy as jnp
from jax import lax
from jax.experimental import pallas as pl
from jax.experimental.pallas import tpu as pltpu
from jax.sharding import Mesh
from jax.sharding import PartitionSpec as P

HEADS = 32
KV_HEADS = 8
HD = 128
GROUP = HEADS // KV_HEADS
NY, NX, NC, NZ = 8, 4, 2, 8
ROW = NX * NC
AXES = ("y", "x", "core", "head")
SEQ = ("y", "x", "core")
F32 = jnp.float32
BF16 = jnp.bfloat16
TOK = 256
FEAT = 512
WROWS = 64
WCOLS = 768
SUBS = 4
SUB = TOK // SUBS
HALF = NZ // 2
CUT = 64
REST = NC * WROWS - CUT


def halves(start, rows):
    first = (rows // 2 + 15) // 16 * 16
    return ((start, first), (start + first, rows - first))


CORE0 = (
    "near", (1, 0), 0, "far", 1, (1, 1), (1, 3), (2, 0), 2, 3, (1, 2), (2, 1), (2, 3), 4, (3, 0), 5,
    (2, 2), (3, 1), 6, (3, 3), 7, (4, 0), 8, (3, 2), 9, (4, 1), (4, 3), 10, (4, 2), 11,
)
CORE1 = (
    "y1", 0, "m0", 1, "y2", 2, "m-1", "m1", "e0", 3, "y3", 4, "e-1", "e1", "m-2", "m2", 5, 6,
    "y4", 7, "e-2", "e2", "m-3", "m3", 8, 9, "e-3", "e3", "m4", 10, 11, "e4",
)
FAR_FIRST = (4, 3, 5, 2, 6, 1, 7)
PARTS = (
    ((0, CUT),) + halves(0, CUT),
    ((CUT, REST),) + halves(CUT, REST),
)
R_ORDER = (0, 1, 2, 3)
L_ORDER = (2, 3, 0, 1)
R_LAST = (0, 1)
L_LAST = (2, 3)
X_ORDER = (0, 1, 3, 2)
XR_LAST = (0, 1)
XL_LAST = (3, 2)


def nt(a, b):
    return lax.dot_general(a, b, (((1,), (1,)), ((), ())), preferred_element_type=F32)


def tn(a, b):
    return lax.dot_general(a, b, (((0,), (0,)), ((), ())), preferred_element_type=F32)


def nn(a, b):
    return jnp.dot(a, b, preferred_element_type=F32)


def kernel(
    a_ref, go_ref, wq_ref, wk_ref, wv_ref, o_ref,
    act, wts, acc, qkv, dq, dk, dv, grads, part, tx, rx,
    st, in1, tot, in2, out3, in3,
    g_ref, o_buf, i_sem, z_send, z_recv, w_send, w_recv, s_send, s_recv, e_send, e_recv, r_send, r_recv,
):
    y, x, c, z = (lax.axis_index(n) for n in AXES)
    r = x * NC + c
    n_y = lambda d: lax.rem(y + d + NY, NY)
    n_x = lambda d: lax.rem(x + d + NX, NX)
    n_z = lambda d: lax.rem(z + d + NZ, NZ)
    n_r = lambda d: lax.rem(r + d + ROW, ROW)
    zr, zl = {"head": n_z(1)}, {"head": n_z(-1)}
    yr, yl = {"y": n_y(1)}, {"y": n_y(-1)}
    xr, xl = {"x": n_x(1)}, {"x": n_x(-1)}
    sib = {"core": 1 - c}
    row_peer = lambda d: {"x": n_r(d) // NC, "core": lax.rem(n_r(d), NC)}

    barrier = pltpu.get_barrier_semaphore()
    peers = [zr, zl] + [row_peer(d) for d in range(1, ROW)] + [{"y": n_y(d)} for d in range(1, NY)]
    for peer in peers:
        pl.semaphore_signal(barrier, inc=1, device_id=peer, device_id_type=pl.DeviceIdType.MESH)

    own = pl.ds(pl.multiple_of(c * WROWS, WROWS), WROWS)
    loads = [
        pltpu.make_async_copy(a_ref, act.at[z], i_sem.at[0]),
        pltpu.make_async_copy(wq_ref, wts.at[y, x, own, pl.ds(0, 512)], i_sem.at[1]),
        pltpu.make_async_copy(wk_ref, wts.at[y, x, own, pl.ds(512, 128)], i_sem.at[2]),
        pltpu.make_async_copy(wv_ref, wts.at[y, x, own, pl.ds(640, 128)], i_sem.at[3]),
        pltpu.make_async_copy(go_ref, g_ref, i_sem.at[4]),
    ]
    for load in loads:
        load.start()
    for load in loads:
        load.wait()
    pl.semaphore_wait(barrier, len(peers))

    def copy(src, dst, ssem, rsem, dev):
        return pltpu.make_async_remote_copy(
            src_ref=src, dst_ref=dst, send_sem=ssem, recv_sem=rsem,
            device_id=dev, device_id_type=pl.DeviceIdType.MESH,
        )

    def same(ref, ssem, rsem, dev):
        return copy(ref, ref, ssem, rsem, dev)

    def z_msg(d, k, s):
        origin = n_z(1 - k) if d == 0 else n_z(k - 1)
        ref = act.at[origin, pl.ds(s * SUB, SUB)]
        return same(ref, z_send.at[d, k, s], z_recv.at[d, k, s], zr if d == 0 else zl)

    def z_wait(d, k, s):
        origin = n_z(-k) if d == 0 else n_z(k)
        ref = act.at[origin, pl.ds(s * SUB, SUB)]
        same(ref, z_send.at[d, k, s], z_recv.at[d, k, s], zr if d == 0 else zl).wait_recv()

    def z_has(d, k, s):
        return k < HALF or (k == HALF and s in (R_LAST if d == 0 else L_LAST))

    def z_start():
        for i in range(SUBS):
            z_msg(0, 1, R_ORDER[i]).start()
            z_msg(1, 1, L_ORDER[i]).start()

    z_ticks = []
    for k in range(1, HALF + 1):
        for i in range(SUBS):
            pair = [(0, k, R_ORDER[i]), (1, k, L_ORDER[i])]
            pair = [p for p in pair if z_has(*p)]
            if pair:
                z_ticks.append(pair)

    def z_tick(i):
        for d, k, s in z_ticks[i]:
            z_wait(d, k, s)
            if z_has(d, k + 1, s):
                z_msg(d, k + 1, s).start()

    def w_ref(dy, dx, core, half=None):
        first, rows = PARTS[core][0 if half is None else 1 + half]
        return wts.at[n_y(dy), n_x(dx), pl.ds(first, rows)]

    def w_msg(ref, i, dev):
        return same(ref, w_send.at[i], w_recv.at[i], dev)

    def sib_ref(m, core):
        return wts.at[n_y(m), :, pl.ds(PARTS[core][0][0], PARTS[core][0][1])]

    def sib_msg(m, core):
        return same(sib_ref(m, core), s_send.at[m % NY], s_recv.at[m % NY], sib)

    def lend_msg():
        ref = wts.at[y, x, pl.ds(CUT, WROWS - CUT)]
        return same(ref, s_send.at[NY], s_recv.at[NY], sib)

    def core0():
        slot = lambda d, k, j: 4 + (d * 5 + k) * 4 + j

        def has(d, k, j):
            return k < 4 or (k == 4 and j in (XR_LAST if d == 0 else XL_LAST))

        def y_msg(d, k, j):
            dy = (1 - k) if d == 0 else (k - 1)
            return w_msg(w_ref(dy, j, 0), slot(d, k, j), yr if d == 0 else yl)

        def y_wait(d, k, j):
            dy = -k if d == 0 else k
            w_msg(w_ref(dy, j, 0), slot(d, k, j), yr if d == 0 else yl).wait_recv()

        def y_both(j):
            y_msg(0, 1, j).start()
            y_msg(1, 1, j).start()

        def x_near():
            w_msg(w_ref(0, 1, 0), 1, xl).wait_recv()
            w_msg(w_ref(0, 1, 0, 1), 3, xl).start()
            y_both(1)
            w_msg(w_ref(0, -1, 0), 0, xr).wait_recv()
            w_msg(w_ref(0, -1, 0, 0), 2, xr).start()
            y_both(3)

        def x_far():
            w_msg(w_ref(0, -2, 0, 0), 2, xr).wait_recv()
            w_msg(w_ref(0, 2, 0, 1), 3, xl).wait_recv()
            y_both(2)
            sib_msg(0, 0).start()

        def y_event(k, j):
            for d in (0, 1):
                if has(d, k, j):
                    y_wait(d, k, j)
                    if has(d, k + 1, j):
                        y_msg(d, k + 1, j).start()
            if j == 2:
                for m in (-k, k) if k < 4 else (4,):
                    sib_msg(m, 0).start()

        if CUT < WROWS:
            lend_msg().start()
        w_msg(w_ref(0, 0, 0), 0, xr).start()
        w_msg(w_ref(0, 0, 0), 1, xl).start()
        y_both(0)
        z_start()
        for step in CORE0:
            if step == "near":
                x_near()
            elif step == "far":
                x_far()
            elif isinstance(step, int):
                z_tick(step)
            else:
                y_event(*step)

        if CUT < WROWS:
            lend_msg().wait_send()
        for i in range(4):
            dx, half, dev = ((0, None, xr), (0, None, xl), (-1, 0, xr), (1, 1, xl))[i]
            w_msg(w_ref(0, dx, 0, half), i, dev).wait_send()
        for k in range(1, 5):
            for j in range(4):
                for d in (0, 1):
                    if has(d, k, j):
                        y_msg(d, k, j).wait_send()

    def core1():
        def y_msg(d, k):
            dy = (1 - k) if d == 0 else (k - 1)
            half = None if k < 4 else d
            return w_msg(w_ref(dy, 0, 1, half), d * 5 + k, yr if d == 0 else yl)

        def y_wait(d, k):
            dy = -k if d == 0 else k
            half = None if k < 4 else d
            w_msg(w_ref(dy, 0, 1, half), d * 5 + k, yr if d == 0 else yl).wait_recv()

        def x_first(m):
            i = 10 + (m % NY) * 4
            return [w_msg(w_ref(m, 0, 1), i, xr), w_msg(w_ref(m, 0, 1), i + 1, xl)]

        def x_second(m, d):
            i = 10 + (m % NY) * 4
            return w_msg(w_ref(m, 2 * d - 1, 1, d), i + 2 + d, xl if d else xr)

        def x_send(m):
            for msg in x_first(m):
                msg.start()

        def x_mid(m):
            i = 10 + (m % NY) * 4
            w_msg(w_ref(m, -1, 1), i, xr).wait_recv()
            x_second(m, 0).start()
            w_msg(w_ref(m, 1, 1), i + 1, xl).wait_recv()
            x_second(m, 1).start()

        def x_end(m):
            i = 10 + (m % NY) * 4
            w_msg(w_ref(m, -2, 1, 0), i + 2, xr).wait_recv()
            w_msg(w_ref(m, 2, 1, 1), i + 3, xl).wait_recv()
            sib_msg(m, 1).start()

        def y_event(k):
            for d in (0, 1):
                y_wait(d, k)
                if k < 4:
                    y_msg(d, k + 1).start()
                    x_send(-k if d == 0 else k)
            if k == 4:
                x_send(4)

        z_start()
        if CUT < WROWS:
            lend_msg().wait_recv()
        y_msg(0, 1).start()
        y_msg(1, 1).start()
        x_send(0)
        for step in CORE1:
            if isinstance(step, int):
                z_tick(step)
            else:
                (y_event, x_mid, x_end)["yme".index(step[0])](int(step[1:]))
        for d in (0, 1):
            for k in range(1, 5):
                y_msg(d, k).wait_send()
        for m in range(NY):
            for msg in x_first(m) + [x_second(m, 0), x_second(m, 1)]:
                msg.wait_send()

    pl.when(c == 0)(core0)
    pl.when(c == 1)(core1)

    def sib_wait(m):
        def wait_for(core):
            same(sib_ref(m, core), s_send.at[m], s_recv.at[m], sib).wait_recv()

        pl.when(c == 0)(lambda: wait_for(1))
        pl.when(c == 1)(lambda: wait_for(0))

    def sib_sent(m):
        pl.when(c == 0)(lambda: sib_msg(m, 0).wait_send())
        pl.when(c == 1)(lambda: sib_msg(m, 1).wait_send())

    far_y, far_z = n_y(4), n_z(4)

    def project(f):
        acc[...] += nn(act[f], wts[f].reshape(FEAT, WCOLS))

    acc[...] = jnp.zeros_like(acc)
    for m in range(NY):
        if m != 4:
            sib_wait(m)

    @pl.loop(0, NZ)
    def _(f):
        @pl.when(jnp.logical_and(f != far_y, f != far_z))
        def _():
            project(f)

    z_tick(12)
    z_tick(13)
    sib_wait(4)
    project(far_y)

    @pl.when(far_y != far_z)
    def _():
        project(far_z)

    for m in range(NY):
        sib_sent(m)
    for pair in [(d, k, s) for d in (0, 1) for k in range(1, HALF + 1) for s in range(SUBS)]:
        if z_has(*pair):
            z_msg(*pair).wait_send()

    qkv[...] = acc[...].astype(BF16)
    head = lambda h: pl.ds(h * HD, HD)
    k_val, v_val = qkv[:, 512:640], qkv[:, 640:768]
    factor = HD ** -0.5
    kv = tn(k_val, v_val)
    gs = tn(qkv[:, head(0)], g_ref[:, head(0)])
    for h in range(1, GROUP):
        gs += tn(qkv[:, head(h)], g_ref[:, head(h)])
    st[:, 0] = kv.astype(BF16).reshape(ROW, HD // ROW, HD)
    st[:, 1] = (factor * gs).astype(BF16).reshape(ROW, HD // ROW, HD)

    def e1(d):
        return copy(st.at[n_r(d)], in1.at[r], e_send.at[0, d], e_recv.at[0, d], row_peer(d))

    def e1_wait(d):
        copy(st.at[r], in1.at[n_r(-d)], e_send.at[0, d], e_recv.at[0, d], row_peer(d)).wait_recv()

    for d in FAR_FIRST:
        e1(d).start()
    in1[r] = st[r]
    rows_t = lax.broadcasted_iota(jnp.int32, (TOK, TOK), 0)
    cols_s = lax.broadcasted_iota(jnp.int32, (TOK, TOK), 1)
    causal = rows_t >= cols_s

    def attend(h):
        q_h, g_h = qkv[:, head(h)], g_ref[:, head(h)]
        k_v, v_v = qkv[:, 512:640], qkv[:, 640:768]
        s = jnp.where(causal, nt(q_h, k_v), 0.0).astype(BF16)
        gsc = jnp.where(causal, nt(g_h, v_v), 0.0).astype(BF16)
        dq[:, head(h)] = nn(gsc, k_v)
        if h == 0:
            dk[...] = tn(gsc, q_h)
            dv[...] = tn(s, g_h)
        else:
            dk[...] += tn(gsc, q_h)
            dv[...] += tn(s, g_h)

    attend(0)
    for d in range(1, ROW):
        e1_wait(d)
    pieces = [in1[i].astype(F32) for i in range(ROW)]
    total = pieces[0]
    for i in range(1, ROW):
        total = total + pieces[i]
    tot[...] = total.astype(BF16)

    def e2(d):
        kind = jnp.where(y + d < NY, 0, 1)
        return copy(tot.at[kind], in2.at[y, kind], e_send.at[1, d], e_recv.at[1, d], {"y": n_y(d)})

    def e2_wait(d):
        kind = jnp.where(y - d >= 0, 0, 1)
        copy(tot.at[kind], in2.at[n_y(-d), kind], e_send.at[1, d], e_recv.at[1, d], {"y": n_y(d)}).wait_recv()

    for d in FAR_FIRST:
        e2(d).start()
    in2[y] = jnp.zeros_like(tot)
    attend(1)
    attend(2)
    for d in range(1, NY):
        e2_wait(d)
    before = jnp.zeros((HD // ROW, HD), F32)
    after = jnp.zeros((HD // ROW, HD), F32)
    for i in range(NY):
        one = in2[i, jnp.where(i < y, 0, 1)].astype(F32)
        before = before + jnp.where(i < y, one, 0.0)
        after = after + jnp.where(i > y, one, 0.0)
    for i in range(ROW):
        out3[i, 0] = before.astype(BF16)
        before = before + pieces[i][0]
    for i in reversed(range(ROW)):
        out3[i, 1] = after.astype(BF16)
        after = after + pieces[i][1]

    def e3(d):
        return copy(out3.at[n_r(d)], in3.at[r], e_send.at[2, d], e_recv.at[2, d], row_peer(d))

    def e3_wait(d):
        copy(out3.at[r], in3.at[n_r(-d)], e_send.at[2, d], e_recv.at[2, d], row_peer(d)).wait_recv()

    for d in FAR_FIRST:
        e3(d).start()
    in3[r] = out3[r]
    attend(3)
    for d in range(1, ROW):
        e3_wait(d)
    for d in range(1, ROW):
        e1(d).wait_send()
        e2(d).wait_send()
        e3(d).wait_send()
    prefix = in3[:, 0].reshape(HD, HD)
    suffix = in3[:, 1].reshape(HD, HD)
    for h in range(GROUP):
        cross = nt(g_ref[:, head(h)], prefix)
        grads[:, head(h)] = (factor * (dq[:, head(h)] + cross)).astype(BF16)
    grads[:, 512:640] = (factor * dk[...] + nt(qkv[:, 640:768], suffix)).astype(BF16)
    grads[:, 640:768] = (factor * dv[...] + nn(qkv[:, 512:640], suffix)).astype(BF16)

    def share(dz, slot):
        part[slot] = nt(grads[...], wts[n_z(dz)].reshape(FEAT, WCOLS))

    def r_msg(d, k, s):
        ds = pl.ds(s * SUB, SUB)
        return copy(tx.at[d, k - 1, ds], rx.at[d, k - 1, ds], r_send.at[d, k, s], r_recv.at[d, k, s], zr if d == 0 else zl)

    def r_step(d, k, s):
        ds = pl.ds(s * SUB, SUB)
        value = part[d, ds]
        if z_has(d, k + 1, s):
            r_msg(d, k + 1, s).wait_recv()
            value = value + rx[d, k, ds].astype(F32)
        tx[d, k - 1, ds] = value.astype(BF16)
        r_msg(d, k, s).start()

    share(HALF, 0)
    for d in (0, 1):
        for s in (R_LAST if d == 0 else L_LAST):
            ds = pl.ds(s * SUB, SUB)
            tx[d, HALF - 1, ds] = part[0, ds].astype(BF16)
            r_msg(d, HALF, s).start()
    for k in range(HALF - 1, 0, -1):
        share(k, 0)
        share(-k, 1)
        for i in range(SUBS):
            r_step(0, k, L_ORDER[i])
            r_step(1, k, R_ORDER[i])
    share(0, 0)

    def out_copy(s):
        ds = pl.ds(s * SUB, SUB)
        return pltpu.make_async_copy(o_buf.at[ds], o_ref.at[ds], i_sem.at[5 + s])

    for i in range(SUBS):
        s = L_ORDER[i]
        ds = pl.ds(s * SUB, SUB)
        r_msg(0, 1, s).wait_recv()
        r_msg(1, 1, s).wait_recv()
        total = part[0, ds] + rx[0, 0, ds].astype(F32) + rx[1, 0, ds].astype(F32)
        o_buf[ds] = total.astype(BF16)
        out_copy(s).start()
    for s in range(SUBS):
        out_copy(s).wait()
    for d in (0, 1):
        for k in range(1, HALF + 1):
            for s in range(SUBS):
                if z_has(d, k, s):
                    r_msg(d, k, s).wait_send()


def local(activations, grad_out, query_weight, key_weight, value_weight):
    dma = pltpu.SemaphoreType.DMA
    return pl.pallas_call(
        kernel,
        out_shape=jax.ShapeDtypeStruct((TOK, FEAT), BF16),
        in_specs=[pl.BlockSpec(memory_space=pltpu.HBM)] * 5,
        out_specs=pl.BlockSpec(memory_space=pltpu.HBM),
        scratch_shapes=[
            pltpu.VMEM((NZ, TOK, FEAT), BF16),
            pltpu.VMEM((NY, NX, NC * WROWS, WCOLS), BF16),
            pltpu.VMEM((TOK, WCOLS), F32),
            pltpu.VMEM((TOK, WCOLS), BF16),
            pltpu.VMEM((TOK, FEAT), F32),
            pltpu.VMEM((TOK, HD), F32),
            pltpu.VMEM((TOK, HD), F32),
            pltpu.VMEM((TOK, WCOLS), BF16),
            pltpu.VMEM((2, TOK, FEAT), F32),
            pltpu.VMEM((2, HALF, TOK, FEAT), BF16),
            pltpu.VMEM((2, HALF, TOK, FEAT), BF16),
            pltpu.VMEM((ROW, 2, HD // ROW, HD), BF16),
            pltpu.VMEM((ROW, 2, HD // ROW, HD), BF16),
            pltpu.VMEM((2, HD // ROW, HD), BF16),
            pltpu.VMEM((NY, 2, HD // ROW, HD), BF16),
            pltpu.VMEM((ROW, 2, HD // ROW, HD), BF16),
            pltpu.VMEM((ROW, 2, HD // ROW, HD), BF16),
            pltpu.VMEM((TOK, FEAT), BF16),
            pltpu.VMEM((TOK, FEAT), BF16),
            dma((5 + SUBS,)),
            dma((2, HALF + 1, SUBS)),
            dma((2, HALF + 1, SUBS)),
            dma((44,)),
            dma((44,)),
            dma((NY + 1,)),
            dma((NY + 1,)),
            dma((3, 8)),
            dma((3, 8)),
            dma((2, HALF + 1, SUBS)),
            dma((2, HALF + 1, SUBS)),
        ],
        compiler_params=pltpu.CompilerParams(
            collective_id=0, has_side_effects=True, vmem_limit_bytes=62 * 1024 * 1024
        ),
        cost_estimate=pl.CostEstimate(flops=4_000_000_000, bytes_accessed=2_000_000, transcendentals=0),
    )(activations, grad_out, query_weight, key_weight, value_weight)


def solution(mesh):
    finer = Mesh(mesh.devices.reshape(NY, NX, NC, NZ), AXES)
    spec = P(SEQ, "head")
    return jax.shard_map(
        local, mesh=finer, in_specs=(spec,) * 5, out_specs=spec, check_vma=False
    )
```

```python
import jax
import jax.numpy as jnp
from jax import lax
from jax.experimental import pallas as pl
from jax.experimental.pallas import tpu as pltpu
from jax.sharding import Mesh
from jax.sharding import PartitionSpec as P

HEADS = 32
KV_HEADS = 8
HD = 128
GROUP = HEADS // KV_HEADS
NY, NX, NC, NZ = 8, 4, 2, 8
ROW = NX * NC
AXES = ("y", "x", "core", "head")
SEQ = ("y", "x", "core")
F32 = jnp.float32
BF16 = jnp.bfloat16
TOK = 256
FEAT = 512
WROWS = 64
WCOLS = 768
SUBS = 4
SUB = TOK // SUBS
HALF = NZ // 2
CUT = 64
REST = NC * WROWS - CUT


def halves(start, rows):
    first = (rows // 2 + 15) // 16 * 16
    return ((start, first), (start + first, rows - first))


CORE0 = (
    "near", (1, 0), 0, "far", 1, (1, 1), (1, 3), (2, 0), 2, 3, (1, 2), (2, 1), (2, 3), 4, (3, 0), 5,
    (2, 2), (3, 1), 6, (3, 3), 7, (4, 0), 8, (3, 2), 9, (4, 1), (4, 3), 10, (4, 2), 11,
)
CORE1 = (
    "y1", 0, "m0", 1, "y2", 2, "m-1", "m1", "e0", 3, "y3", 4, "e-1", "e1", "m-2", "m2", 5, 6,
    "y4", 7, "e-2", "e2", "m-3", "m3", 8, 9, "e-3", "e3", "m4", 10, 11, "e4",
)
PIECES = 2
PIECE = TOK // PIECES
R_TURN = tuple(range(PIECES))
R_PART, L_PART = R_TURN[: PIECES // 2], R_TURN[PIECES // 2 :]
L_TURN = L_PART + R_PART
FAR_FIRST = (4, 3, 5, 2, 6, 1, 7)
PARTS = (
    ((0, CUT),) + halves(0, CUT),
    ((CUT, REST),) + halves(CUT, REST),
)
R_ORDER = (0, 1, 2, 3)
L_ORDER = (2, 3, 0, 1)
R_LAST = (0, 1)
L_LAST = (2, 3)
X_ORDER = (0, 1, 3, 2)
XR_LAST = (0, 1)
XL_LAST = (3, 2)


def nt(a, b):
    return lax.dot_general(a, b, (((1,), (1,)), ((), ())), preferred_element_type=F32)


def tn(a, b):
    return lax.dot_general(a, b, (((0,), (0,)), ((), ())), preferred_element_type=F32)


def nn(a, b):
    return jnp.dot(a, b, preferred_element_type=F32)


def kernel(
    a_ref, go_ref, wq_ref, wk_ref, wv_ref, o_ref,
    act, wts, acc, qkv, dq, dk, dv, grads, part, tx, rx,
    st, in1, tot, in2, out3, in3,
    g_ref, i_sem, z_send, z_recv, w_send, w_recv, s_send, s_recv, e_send, e_recv, r_send, r_recv,
):
    y, x, c, z = (lax.axis_index(n) for n in AXES)
    r = x * NC + c
    n_y = lambda d: lax.rem(y + d + NY, NY)
    n_x = lambda d: lax.rem(x + d + NX, NX)
    n_z = lambda d: lax.rem(z + d + NZ, NZ)
    n_r = lambda d: lax.rem(r + d + ROW, ROW)
    zr, zl = {"head": n_z(1)}, {"head": n_z(-1)}
    yr, yl = {"y": n_y(1)}, {"y": n_y(-1)}
    xr, xl = {"x": n_x(1)}, {"x": n_x(-1)}
    sib = {"core": 1 - c}
    row_peer = lambda d: {"x": n_r(d) // NC, "core": lax.rem(n_r(d), NC)}

    own = pl.ds(pl.multiple_of(c * WROWS, WROWS), WROWS)
    loads = [
        pltpu.make_async_copy(a_ref, act.at[z], i_sem.at[0]),
        pltpu.make_async_copy(wq_ref, wts.at[y, x, own, pl.ds(0, 512)], i_sem.at[1]),
        pltpu.make_async_copy(wk_ref, wts.at[y, x, own, pl.ds(512, 128)], i_sem.at[2]),
        pltpu.make_async_copy(wv_ref, wts.at[y, x, own, pl.ds(640, 128)], i_sem.at[3]),
        pltpu.make_async_copy(go_ref, g_ref, i_sem.at[4]),
    ]
    for load in loads:
        load.start()
    barrier = pltpu.get_barrier_semaphore()
    peers = [zr, zl] + [row_peer(d) for d in range(1, ROW)] + [{"y": n_y(d)} for d in range(1, NY)]
    for peer in peers:
        pl.semaphore_signal(barrier, inc=1, device_id=peer, device_id_type=pl.DeviceIdType.MESH)

    pl.semaphore_wait(barrier, len(peers))
    for load in loads[1:4]:
        load.wait()

    def copy(src, dst, ssem, rsem, dev):
        return pltpu.make_async_remote_copy(
            src_ref=src, dst_ref=dst, send_sem=ssem, recv_sem=rsem,
            device_id=dev, device_id_type=pl.DeviceIdType.MESH,
        )

    def same(ref, ssem, rsem, dev):
        return copy(ref, ref, ssem, rsem, dev)

    def z_msg(d, k, s):
        origin = n_z(1 - k) if d == 0 else n_z(k - 1)
        ref = act.at[origin, pl.ds(s * SUB, SUB)]
        if k == 1:
            return copy(
                a_ref.at[pl.ds(s * SUB, SUB)], ref, z_send.at[d, k, s], z_recv.at[d, k, s],
                zr if d == 0 else zl,
            )
        return same(ref, z_send.at[d, k, s], z_recv.at[d, k, s], zr if d == 0 else zl)

    def z_wait(d, k, s):
        origin = n_z(-k) if d == 0 else n_z(k)
        ref = act.at[origin, pl.ds(s * SUB, SUB)]
        same(ref, z_send.at[d, k, s], z_recv.at[d, k, s], zr if d == 0 else zl).wait_recv()

    def z_has(d, k, s):
        return k < HALF or (k == HALF and s in (R_LAST if d == 0 else L_LAST))

    def z_start():
        for i in range(SUBS):
            z_msg(0, 1, R_ORDER[i]).start()
            z_msg(1, 1, L_ORDER[i]).start()

    z_ticks = []
    for k in range(1, HALF + 1):
        for i in range(SUBS):
            pair = [(0, k, R_ORDER[i]), (1, k, L_ORDER[i])]
            pair = [p for p in pair if z_has(*p)]
            if pair:
                z_ticks.append(pair)

    def z_tick(i):
        for d, k, s in z_ticks[i]:
            z_wait(d, k, s)
            if z_has(d, k + 1, s):
                z_msg(d, k + 1, s).start()

    def w_ref(dy, dx, core, half=None):
        first, rows = PARTS[core][0 if half is None else 1 + half]
        return wts.at[n_y(dy), n_x(dx), pl.ds(first, rows)]

    def w_msg(ref, i, dev):
        return same(ref, w_send.at[i], w_recv.at[i], dev)

    def sib_ref(m, core):
        return wts.at[n_y(m), :, pl.ds(PARTS[core][0][0], PARTS[core][0][1])]

    def sib_msg(m, core):
        return same(sib_ref(m, core), s_send.at[m % NY], s_recv.at[m % NY], sib)

    def lend_msg():
        ref = wts.at[y, x, pl.ds(CUT, WROWS - CUT)]
        return same(ref, s_send.at[NY], s_recv.at[NY], sib)

    def core0():
        slot = lambda d, k, j: 4 + (d * 5 + k) * 4 + j

        def has(d, k, j):
            return k < 4 or (k == 4 and j in (XR_LAST if d == 0 else XL_LAST))

        def y_msg(d, k, j):
            dy = (1 - k) if d == 0 else (k - 1)
            return w_msg(w_ref(dy, j, 0), slot(d, k, j), yr if d == 0 else yl)

        def y_wait(d, k, j):
            dy = -k if d == 0 else k
            w_msg(w_ref(dy, j, 0), slot(d, k, j), yr if d == 0 else yl).wait_recv()

        def y_both(j):
            y_msg(0, 1, j).start()
            y_msg(1, 1, j).start()

        def x_near():
            w_msg(w_ref(0, 1, 0), 1, xl).wait_recv()
            w_msg(w_ref(0, 1, 0, 1), 3, xl).start()
            y_both(1)
            w_msg(w_ref(0, -1, 0), 0, xr).wait_recv()
            w_msg(w_ref(0, -1, 0, 0), 2, xr).start()
            y_both(3)

        def x_far():
            w_msg(w_ref(0, -2, 0, 0), 2, xr).wait_recv()
            w_msg(w_ref(0, 2, 0, 1), 3, xl).wait_recv()
            y_both(2)
            sib_msg(0, 0).start()

        def y_event(k, j):
            for d in (0, 1):
                if has(d, k, j):
                    y_wait(d, k, j)
                    if has(d, k + 1, j):
                        y_msg(d, k + 1, j).start()
            if j == 2:
                for m in (-k, k) if k < 4 else (4,):
                    sib_msg(m, 0).start()

        if CUT < WROWS:
            lend_msg().start()
        w_msg(w_ref(0, 0, 0), 0, xr).start()
        w_msg(w_ref(0, 0, 0), 1, xl).start()
        y_both(0)
        z_start()
        for step in CORE0:
            if step == "near":
                x_near()
            elif step == "far":
                x_far()
            elif isinstance(step, int):
                z_tick(step)
            else:
                y_event(*step)

        if CUT < WROWS:
            lend_msg().wait_send()
        for i in range(4):
            dx, half, dev = ((0, None, xr), (0, None, xl), (-1, 0, xr), (1, 1, xl))[i]
            w_msg(w_ref(0, dx, 0, half), i, dev).wait_send()
        for k in range(1, 5):
            for j in range(4):
                for d in (0, 1):
                    if has(d, k, j):
                        y_msg(d, k, j).wait_send()

    def core1():
        def y_msg(d, k):
            dy = (1 - k) if d == 0 else (k - 1)
            half = None if k < 4 else d
            return w_msg(w_ref(dy, 0, 1, half), d * 5 + k, yr if d == 0 else yl)

        def y_wait(d, k):
            dy = -k if d == 0 else k
            half = None if k < 4 else d
            w_msg(w_ref(dy, 0, 1, half), d * 5 + k, yr if d == 0 else yl).wait_recv()

        def x_first(m):
            i = 10 + (m % NY) * 4
            return [w_msg(w_ref(m, 0, 1), i, xr), w_msg(w_ref(m, 0, 1), i + 1, xl)]

        def x_second(m, d):
            i = 10 + (m % NY) * 4
            return w_msg(w_ref(m, 2 * d - 1, 1, d), i + 2 + d, xl if d else xr)

        def x_send(m):
            for msg in x_first(m):
                msg.start()

        def x_mid(m):
            i = 10 + (m % NY) * 4
            w_msg(w_ref(m, -1, 1), i, xr).wait_recv()
            x_second(m, 0).start()
            w_msg(w_ref(m, 1, 1), i + 1, xl).wait_recv()
            x_second(m, 1).start()

        def x_end(m):
            i = 10 + (m % NY) * 4
            w_msg(w_ref(m, -2, 1, 0), i + 2, xr).wait_recv()
            w_msg(w_ref(m, 2, 1, 1), i + 3, xl).wait_recv()
            sib_msg(m, 1).start()

        def y_event(k):
            for d in (0, 1):
                y_wait(d, k)
                if k < 4:
                    y_msg(d, k + 1).start()
                    x_send(-k if d == 0 else k)
            if k == 4:
                x_send(4)

        z_start()
        if CUT < WROWS:
            lend_msg().wait_recv()
        y_msg(0, 1).start()
        y_msg(1, 1).start()
        x_send(0)
        for step in CORE1:
            if isinstance(step, int):
                z_tick(step)
            else:
                (y_event, x_mid, x_end)["yme".index(step[0])](int(step[1:]))
        for d in (0, 1):
            for k in range(1, 5):
                y_msg(d, k).wait_send()
        for m in range(NY):
            for msg in x_first(m) + [x_second(m, 0), x_second(m, 1)]:
                msg.wait_send()

    pl.when(c == 0)(core0)
    pl.when(c == 1)(core1)

    def sib_wait(m):
        def wait_for(core):
            same(sib_ref(m, core), s_send.at[m], s_recv.at[m], sib).wait_recv()

        pl.when(c == 0)(lambda: wait_for(1))
        pl.when(c == 1)(lambda: wait_for(0))

    def sib_sent(m):
        pl.when(c == 0)(lambda: sib_msg(m, 0).wait_send())
        pl.when(c == 1)(lambda: sib_msg(m, 1).wait_send())

    far_y, far_z = n_y(4), n_z(4)

    def project(f):
        acc[...] += nn(act[f], wts[f].reshape(FEAT, WCOLS))

    acc[...] = jnp.zeros_like(acc)
    loads[0].wait()
    loads[4].wait()
    for m in range(NY):
        if m != 4:
            sib_wait(m)

    @pl.loop(0, NZ)
    def _(f):
        @pl.when(jnp.logical_and(f != far_y, f != far_z))
        def _():
            project(f)

    z_tick(12)
    z_tick(13)
    sib_wait(4)
    project(far_y)

    @pl.when(far_y != far_z)
    def _():
        project(far_z)

    for m in range(NY):
        sib_sent(m)
    for pair in [(d, k, s) for d in (0, 1) for k in range(1, HALF + 1) for s in range(SUBS)]:
        if z_has(*pair):
            z_msg(*pair).wait_send()

    qkv[...] = acc[...].astype(BF16)
    head = lambda h: pl.ds(h * HD, HD)
    k_val, v_val = qkv[:, 512:640], qkv[:, 640:768]
    factor = HD ** -0.5
    kv = tn(k_val, v_val)
    gs = tn(qkv[:, head(0)], g_ref[:, head(0)])
    for h in range(1, GROUP):
        gs += tn(qkv[:, head(h)], g_ref[:, head(h)])
    st[:, 0] = kv.astype(BF16).reshape(ROW, HD // ROW, HD)
    st[:, 1] = (factor * gs).astype(BF16).reshape(ROW, HD // ROW, HD)

    def e1(d):
        return copy(st.at[n_r(d)], in1.at[r], e_send.at[0, d], e_recv.at[0, d], row_peer(d))

    def e1_wait(d):
        copy(st.at[r], in1.at[n_r(-d)], e_send.at[0, d], e_recv.at[0, d], row_peer(d)).wait_recv()

    for d in FAR_FIRST:
        e1(d).start()
    in1[r] = st[r]
    rows_t = lax.broadcasted_iota(jnp.int32, (TOK, TOK), 0)
    cols_s = lax.broadcasted_iota(jnp.int32, (TOK, TOK), 1)
    causal = rows_t >= cols_s

    def attend(h):
        q_h, g_h = qkv[:, head(h)], g_ref[:, head(h)]
        k_v, v_v = qkv[:, 512:640], qkv[:, 640:768]
        s = jnp.where(causal, nt(q_h, k_v), 0.0).astype(BF16)
        gsc = jnp.where(causal, nt(g_h, v_v), 0.0).astype(BF16)
        dq[:, head(h)] = nn(gsc, k_v)
        if h == 0:
            dk[...] = tn(gsc, q_h)
            dv[...] = tn(s, g_h)
        else:
            dk[...] += tn(gsc, q_h)
            dv[...] += tn(s, g_h)

    attend(0)
    for d in range(1, ROW):
        e1_wait(d)
    pieces = [in1[i].astype(F32) for i in range(ROW)]
    total = pieces[0]
    for i in range(1, ROW):
        total = total + pieces[i]
    tot[...] = total.astype(BF16)

    def e2(d):
        kind = jnp.where(y + d < NY, 0, 1)
        return copy(tot.at[kind], in2.at[y, kind], e_send.at[1, d], e_recv.at[1, d], {"y": n_y(d)})

    def e2_wait(d):
        kind = jnp.where(y - d >= 0, 0, 1)
        copy(tot.at[kind], in2.at[n_y(-d), kind], e_send.at[1, d], e_recv.at[1, d], {"y": n_y(d)}).wait_recv()

    for d in FAR_FIRST:
        e2(d).start()
    in2[y] = jnp.zeros_like(tot)
    attend(1)
    attend(2)
    for d in range(1, NY):
        e2_wait(d)
    before = jnp.zeros((HD // ROW, HD), F32)
    after = jnp.zeros((HD // ROW, HD), F32)
    for i in range(NY):
        one = in2[i, jnp.where(i < y, 0, 1)].astype(F32)
        before = before + jnp.where(i < y, one, 0.0)
        after = after + jnp.where(i > y, one, 0.0)
    for i in range(ROW):
        out3[i, 0] = before.astype(BF16)
        before = before + pieces[i][0]
    for i in reversed(range(ROW)):
        out3[i, 1] = after.astype(BF16)
        after = after + pieces[i][1]

    def e3(d):
        return copy(out3.at[n_r(d)], in3.at[r], e_send.at[2, d], e_recv.at[2, d], row_peer(d))

    def e3_wait(d):
        copy(out3.at[r], in3.at[n_r(-d)], e_send.at[2, d], e_recv.at[2, d], row_peer(d)).wait_recv()

    for d in FAR_FIRST:
        e3(d).start()
    in3[r] = out3[r]
    attend(3)
    for d in range(1, ROW):
        e3_wait(d)
    for d in range(1, ROW):
        e1(d).wait_send()
        e2(d).wait_send()
        e3(d).wait_send()
    prefix = in3[:, 0].reshape(HD, HD)
    suffix = in3[:, 1].reshape(HD, HD)
    for h in range(GROUP):
        cross = nt(g_ref[:, head(h)], prefix)
        grads[:, head(h)] = (factor * (dq[:, head(h)] + cross)).astype(BF16)
    grads[:, 512:640] = (factor * dk[...] + nt(qkv[:, 640:768], suffix)).astype(BF16)
    grads[:, 640:768] = (factor * dv[...] + nn(qkv[:, 512:640], suffix)).astype(BF16)

    def share(dz, slot):
        part[slot] = nt(grads[...], wts[n_z(dz)].reshape(FEAT, WCOLS))

    def r_has(d, k, s):
        return k < HALF or (k == HALF and s in (R_PART if d == 0 else L_PART))

    def r_msg(d, k, s):
        ds = pl.ds(s * PIECE, PIECE)
        return copy(tx.at[d, k - 1, ds], rx.at[d, k - 1, ds], r_send.at[d, k, s], r_recv.at[d, k, s], zr if d == 0 else zl)

    def r_step(d, k, s):
        ds = pl.ds(s * PIECE, PIECE)
        value = part[d, ds]
        if r_has(d, k + 1, s):
            r_msg(d, k + 1, s).wait_recv()
            value = value + rx[d, k, ds].astype(F32)
        tx[d, k - 1, ds] = value.astype(BF16)
        r_msg(d, k, s).start()

    share(HALF, 0)
    for d in (0, 1):
        for s in (R_PART if d == 0 else L_PART):
            ds = pl.ds(s * PIECE, PIECE)
            tx[d, HALF - 1, ds] = part[0, ds].astype(BF16)
            r_msg(d, HALF, s).start()
    for k in range(HALF - 1, 0, -1):
        share(k, 0)
        share(-k, 1)
        for i in range(PIECES):
            r_step(0, k, L_TURN[i])
            r_step(1, k, R_TURN[i])
    share(0, 0)
    for i in range(PIECES):
        s = L_TURN[i]
        ds = pl.ds(s * PIECE, PIECE)
        r_msg(0, 1, s).wait_recv()
        r_msg(1, 1, s).wait_recv()
        total = part[0, ds] + rx[0, 0, ds].astype(F32) + rx[1, 0, ds].astype(F32)
        o_ref[ds] = total.astype(BF16)
    for d in (0, 1):
        for k in range(1, HALF + 1):
            for s in range(PIECES):
                if r_has(d, k, s):
                    r_msg(d, k, s).wait_send()


def local(activations, grad_out, query_weight, key_weight, value_weight):
    dma = pltpu.SemaphoreType.DMA
    operands = (activations, grad_out, query_weight, key_weight, value_weight)
    operands = [pltpu.with_memory_space_constraint(v, pltpu.HBM) for v in operands]
    return pl.pallas_call(
        kernel,
        out_shape=jax.ShapeDtypeStruct((TOK, FEAT), BF16),
        in_specs=[pl.BlockSpec(memory_space=pltpu.HBM)] * 5,
        out_specs=pl.BlockSpec(memory_space=pltpu.VMEM),
        scratch_shapes=[
            pltpu.VMEM((NZ, TOK, FEAT), BF16),
            pltpu.VMEM((NY, NX, NC * WROWS, WCOLS), BF16),
            pltpu.VMEM((TOK, WCOLS), F32),
            pltpu.VMEM((TOK, WCOLS), BF16),
            pltpu.VMEM((TOK, FEAT), F32),
            pltpu.VMEM((TOK, HD), F32),
            pltpu.VMEM((TOK, HD), F32),
            pltpu.VMEM((TOK, WCOLS), BF16),
            pltpu.VMEM((4, TOK, FEAT), F32),
            pltpu.VMEM((2, HALF, TOK, FEAT), BF16),
            pltpu.VMEM((2, HALF, TOK, FEAT), BF16),
            pltpu.VMEM((ROW, 2, HD // ROW, HD), BF16),
            pltpu.VMEM((ROW, 2, HD // ROW, HD), BF16),
            pltpu.VMEM((2, HD // ROW, HD), BF16),
            pltpu.VMEM((NY, 2, HD // ROW, HD), BF16),
            pltpu.VMEM((ROW, 2, HD // ROW, HD), BF16),
            pltpu.VMEM((ROW, 2, HD // ROW, HD), BF16),
            pltpu.VMEM((TOK, FEAT), BF16),
            dma((5,)),
            dma((2, HALF + 1, SUBS)),
            dma((2, HALF + 1, SUBS)),
            dma((44,)),
            dma((44,)),
            dma((NY + 1,)),
            dma((NY + 1,)),
            dma((3, 8)),
            dma((3, 8)),
            dma((2, HALF + 1, PIECES)),
            dma((2, HALF + 1, PIECES)),
        ],
        compiler_params=pltpu.CompilerParams(
            collective_id=0, has_side_effects=True, vmem_limit_bytes=48 * 1024 * 1024
        ),
        cost_estimate=pl.CostEstimate(flops=4_000_000_000, bytes_accessed=2_000_000, transcendentals=0),
    )(*operands)


def solution(mesh):
    finer = Mesh(mesh.devices.reshape(NY, NX, NC, NZ), AXES)
    spec = P(SEQ, "head")
    return jax.shard_map(
        local, mesh=finer, in_specs=(spec,) * 5, out_specs=spec, check_vma=False
    )
```

```python
import jax
import jax.numpy as jnp
from jax import lax
from jax.experimental import pallas as pl
from jax.experimental.pallas import tpu as pltpu
from jax.sharding import Mesh
from jax.sharding import PartitionSpec as P

HEADS = 32
KV_HEADS = 8
HD = 128
GROUP = HEADS // KV_HEADS
NY, NX, NC, NZ = 8, 4, 2, 8
ROW = NX * NC
AXES = ("y", "x", "core", "head")
SEQ = ("y", "x", "core")
F32 = jnp.float32
BF16 = jnp.bfloat16
TOK = 256
FEAT = 512
WROWS = 64
WCOLS = 768
SUBS = 4
SUB = TOK // SUBS
HALF = NZ // 2
CUT = 64
REST = NC * WROWS - CUT


def halves(start, rows):
    first = (rows // 2 + 15) // 16 * 16
    return ((start, first), (start + first, rows - first))


CORE0 = (
    "near", (1, 0), 0, "far", 1, (1, 1), (1, 3), (2, 0), 2, 3, (1, 2), (2, 1), (2, 3), 4, (3, 0), 5,
    (2, 2), (3, 1), 6, (3, 3), 7, (4, 0), 8, (3, 2), 9, (4, 1), (4, 3), 10, (4, 2), 11,
)
CORE1 = (
    "y1", 0, "m0", 1, "y2", 2, "m-1", "m1", "e0", 3, "y3", 4, "e-1", "e1", "m-2", "m2", 5, 6,
    "y4", 7, "e-2", "e2", "m-3", "m3", 8, 9, "e-3", "e3", "m4", 10, 11, "e4",
)
PIECES = 2
PIECE = TOK // PIECES
R_TURN = tuple(range(PIECES))
R_PART, L_PART = R_TURN[: PIECES // 2], R_TURN[PIECES // 2 :]
L_TURN = L_PART + R_PART
FAR_FIRST = (4, 3, 5, 2, 6, 1, 7)
PARTS = (
    ((0, CUT),) + halves(0, CUT),
    ((CUT, REST),) + halves(CUT, REST),
)
R_ORDER = (0, 1, 2, 3)
L_ORDER = (2, 3, 0, 1)
R_LAST = (0, 1)
L_LAST = (2, 3)
X_ORDER = (0, 1, 3, 2)
XR_LAST = (0, 1)
XL_LAST = (3, 2)


def nt(a, b):
    return lax.dot_general(a, b, (((1,), (1,)), ((), ())), preferred_element_type=F32)


def tn(a, b):
    return lax.dot_general(a, b, (((0,), (0,)), ((), ())), preferred_element_type=F32)


def nn(a, b):
    return jnp.dot(a, b, preferred_element_type=F32)


def kernel(
    a_ref, go_ref, wq_ref, wk_ref, wv_ref, o_ref,
    act, wts, acc, qkv, dq, dk, dv, grads, part, tx, rx,
    st, in1, tot, in2, out3, in3,
    g_ref, i_sem, z_send, z_recv, w_send, w_recv, s_send, s_recv, e_send, e_recv, r_send, r_recv,
):
    y, x, c, z = (lax.axis_index(n) for n in AXES)
    r = x * NC + c
    n_y = lambda d: lax.rem(y + d + NY, NY)
    n_x = lambda d: lax.rem(x + d + NX, NX)
    n_z = lambda d: lax.rem(z + d + NZ, NZ)
    n_r = lambda d: lax.rem(r + d + ROW, ROW)
    zr, zl = {"head": n_z(1)}, {"head": n_z(-1)}
    yr, yl = {"y": n_y(1)}, {"y": n_y(-1)}
    xr, xl = {"x": n_x(1)}, {"x": n_x(-1)}
    sib = {"core": 1 - c}
    row_peer = lambda d: {"x": n_r(d) // NC, "core": lax.rem(n_r(d), NC)}

    own = pl.ds(pl.multiple_of(c * WROWS, WROWS), WROWS)
    loads = [
        pltpu.make_async_copy(a_ref, act.at[z], i_sem.at[0]),
        pltpu.make_async_copy(wq_ref, wts.at[y, x, own, pl.ds(0, 512)], i_sem.at[1]),
        pltpu.make_async_copy(wk_ref, wts.at[y, x, own, pl.ds(512, 128)], i_sem.at[2]),
        pltpu.make_async_copy(wv_ref, wts.at[y, x, own, pl.ds(640, 128)], i_sem.at[3]),
        pltpu.make_async_copy(go_ref, g_ref, i_sem.at[4]),
    ]
    for load in loads:
        load.start()
    barrier = pltpu.get_barrier_semaphore()
    peers = [zr, zl, yr, yl, xr, xl, sib]
    for peer in peers:
        pl.semaphore_signal(barrier, inc=1, device_id=peer, device_id_type=pl.DeviceIdType.MESH)

    pl.semaphore_wait(barrier, len(peers))
    for load in loads[1:4]:
        load.wait()

    def copy(src, dst, ssem, rsem, dev):
        return pltpu.make_async_remote_copy(
            src_ref=src, dst_ref=dst, send_sem=ssem, recv_sem=rsem,
            device_id=dev, device_id_type=pl.DeviceIdType.MESH,
        )

    def same(ref, ssem, rsem, dev):
        return copy(ref, ref, ssem, rsem, dev)

    def z_msg(d, k, s):
        origin = n_z(1 - k) if d == 0 else n_z(k - 1)
        ref = act.at[origin, pl.ds(s * SUB, SUB)]
        if k == 1:
            return copy(
                a_ref.at[pl.ds(s * SUB, SUB)], ref, z_send.at[d, k, s], z_recv.at[d, k, s],
                zr if d == 0 else zl,
            )
        return same(ref, z_send.at[d, k, s], z_recv.at[d, k, s], zr if d == 0 else zl)

    def z_wait(d, k, s):
        origin = n_z(-k) if d == 0 else n_z(k)
        ref = act.at[origin, pl.ds(s * SUB, SUB)]
        same(ref, z_send.at[d, k, s], z_recv.at[d, k, s], zr if d == 0 else zl).wait_recv()

    def z_has(d, k, s):
        return k < HALF or (k == HALF and s in (R_LAST if d == 0 else L_LAST))

    def z_start():
        for i in range(SUBS):
            z_msg(0, 1, R_ORDER[i]).start()
            z_msg(1, 1, L_ORDER[i]).start()

    z_ticks = []
    for k in range(1, HALF + 1):
        for i in range(SUBS):
            pair = [(0, k, R_ORDER[i]), (1, k, L_ORDER[i])]
            pair = [p for p in pair if z_has(*p)]
            if pair:
                z_ticks.append(pair)

    def z_tick(i):
        for d, k, s in z_ticks[i]:
            z_wait(d, k, s)
            if z_has(d, k + 1, s):
                z_msg(d, k + 1, s).start()

    def w_ref(dy, dx, core, half=None):
        first, rows = PARTS[core][0 if half is None else 1 + half]
        return wts.at[n_y(dy), n_x(dx), pl.ds(first, rows)]

    def w_msg(ref, i, dev):
        return same(ref, w_send.at[i], w_recv.at[i], dev)

    def sib_ref(m, core):
        return wts.at[n_y(m), :, pl.ds(PARTS[core][0][0], PARTS[core][0][1])]

    def sib_msg(m, core):
        return same(sib_ref(m, core), s_send.at[m % NY], s_recv.at[m % NY], sib)

    def lend_msg():
        ref = wts.at[y, x, pl.ds(CUT, WROWS - CUT)]
        return same(ref, s_send.at[NY], s_recv.at[NY], sib)

    def make0():
        slot = lambda d, k, j: 4 + (d * 5 + k) * 4 + j

        def has(d, k, j):
            return k < 4 or (k == 4 and j in (XR_LAST if d == 0 else XL_LAST))

        def y_msg(d, k, j):
            dy = (1 - k) if d == 0 else (k - 1)
            return w_msg(w_ref(dy, j, 0), slot(d, k, j), yr if d == 0 else yl)

        def y_wait(d, k, j):
            dy = -k if d == 0 else k
            w_msg(w_ref(dy, j, 0), slot(d, k, j), yr if d == 0 else yl).wait_recv()

        def y_both(j):
            y_msg(0, 1, j).start()
            y_msg(1, 1, j).start()

        def x_near():
            w_msg(w_ref(0, 1, 0), 1, xl).wait_recv()
            w_msg(w_ref(0, 1, 0, 1), 3, xl).start()
            y_both(1)
            w_msg(w_ref(0, -1, 0), 0, xr).wait_recv()
            w_msg(w_ref(0, -1, 0, 0), 2, xr).start()
            y_both(3)

        def x_far():
            w_msg(w_ref(0, -2, 0, 0), 2, xr).wait_recv()
            w_msg(w_ref(0, 2, 0, 1), 3, xl).wait_recv()
            y_both(2)
            sib_msg(0, 0).start()

        def y_event(k, j):
            for d in (0, 1):
                if has(d, k, j):
                    y_wait(d, k, j)
                    if has(d, k + 1, j):
                        y_msg(d, k + 1, j).start()
            if j == 2:
                for m in (-k, k) if k < 4 else (4,):
                    sib_msg(m, 0).start()

        def run():
            if CUT < WROWS:
                lend_msg().start()
            w_msg(w_ref(0, 0, 0), 0, xr).start()
            w_msg(w_ref(0, 0, 0), 1, xl).start()
            y_both(0)
            z_start()
            for step in CORE0:
                if step == "near":
                    x_near()
                elif step == "far":
                    x_far()
                elif isinstance(step, int):
                    z_tick(step)
                else:
                    y_event(*step)

        def drain():
            if CUT < WROWS:
                lend_msg().wait_send()
            for i in range(4):
                dx, half, dev = ((0, None, xr), (0, None, xl), (-1, 0, xr), (1, 1, xl))[i]
                w_msg(w_ref(0, dx, 0, half), i, dev).wait_send()
            for k in range(1, 5):
                for j in range(4):
                    for d in (0, 1):
                        if has(d, k, j):
                            y_msg(d, k, j).wait_send()

        return run, drain

    def make1():
        def y_msg(d, k):
            dy = (1 - k) if d == 0 else (k - 1)
            half = None if k < 4 else d
            return w_msg(w_ref(dy, 0, 1, half), d * 5 + k, yr if d == 0 else yl)

        def y_wait(d, k):
            dy = -k if d == 0 else k
            half = None if k < 4 else d
            w_msg(w_ref(dy, 0, 1, half), d * 5 + k, yr if d == 0 else yl).wait_recv()

        def x_first(m):
            i = 10 + (m % NY) * 4
            return [w_msg(w_ref(m, 0, 1), i, xr), w_msg(w_ref(m, 0, 1), i + 1, xl)]

        def x_second(m, d):
            i = 10 + (m % NY) * 4
            return w_msg(w_ref(m, 2 * d - 1, 1, d), i + 2 + d, xl if d else xr)

        def x_send(m):
            for msg in x_first(m):
                msg.start()

        def x_mid(m):
            i = 10 + (m % NY) * 4
            w_msg(w_ref(m, -1, 1), i, xr).wait_recv()
            x_second(m, 0).start()
            w_msg(w_ref(m, 1, 1), i + 1, xl).wait_recv()
            x_second(m, 1).start()

        def x_end(m):
            i = 10 + (m % NY) * 4
            w_msg(w_ref(m, -2, 1, 0), i + 2, xr).wait_recv()
            w_msg(w_ref(m, 2, 1, 1), i + 3, xl).wait_recv()
            sib_msg(m, 1).start()

        def y_event(k):
            for d in (0, 1):
                y_wait(d, k)
                if k < 4:
                    y_msg(d, k + 1).start()
                    x_send(-k if d == 0 else k)
            if k == 4:
                x_send(4)

        def run():
            z_start()
            if CUT < WROWS:
                lend_msg().wait_recv()
            y_msg(0, 1).start()
            y_msg(1, 1).start()
            x_send(0)
            for step in CORE1:
                if isinstance(step, int):
                    z_tick(step)
                else:
                    (y_event, x_mid, x_end)["yme".index(step[0])](int(step[1:]))

        def drain():
            for d in (0, 1):
                for k in range(1, 5):
                    y_msg(d, k).wait_send()
            for m in range(NY):
                for msg in x_first(m) + [x_second(m, 0), x_second(m, 1)]:
                    msg.wait_send()

        return run, drain

    run0, drain0 = make0()
    run1, drain1 = make1()
    pl.when(c == 0)(run0)
    pl.when(c == 1)(run1)

    def sib_wait(m):
        def wait_for(core):
            same(sib_ref(m, core), s_send.at[m], s_recv.at[m], sib).wait_recv()

        pl.when(c == 0)(lambda: wait_for(1))
        pl.when(c == 1)(lambda: wait_for(0))

    def sib_sent(m):
        pl.when(c == 0)(lambda: sib_msg(m, 0).wait_send())
        pl.when(c == 1)(lambda: sib_msg(m, 1).wait_send())

    far_y, far_z = n_y(4), n_z(4)

    def project(f):
        acc[...] += nn(act[f], wts[f].reshape(FEAT, WCOLS))

    acc[...] = jnp.zeros_like(acc)
    loads[0].wait()
    loads[4].wait()
    for m in range(NY):
        if m != 4:
            sib_wait(m)

    @pl.loop(0, NZ)
    def _(f):
        @pl.when(jnp.logical_and(f != far_y, f != far_z))
        def _():
            project(f)

    z_tick(12)
    z_tick(13)
    sib_wait(4)
    project(far_y)

    @pl.when(far_y != far_z)
    def _():
        project(far_z)

    qkv[...] = acc[...].astype(BF16)
    head = lambda h: pl.ds(h * HD, HD)
    k_val, v_val = qkv[:, 512:640], qkv[:, 640:768]
    factor = HD ** -0.5
    kv = tn(k_val, v_val)
    gs = tn(qkv[:, head(0)], g_ref[:, head(0)])
    for h in range(1, GROUP):
        gs += tn(qkv[:, head(h)], g_ref[:, head(h)])
    st[:, 0] = kv.astype(BF16).reshape(ROW, HD // ROW, HD)
    st[:, 1] = (factor * gs).astype(BF16).reshape(ROW, HD // ROW, HD)

    def e1(d):
        return copy(st.at[n_r(d)], in1.at[r], e_send.at[0, d], e_recv.at[0, d], row_peer(d))

    def e1_wait(d):
        copy(st.at[r], in1.at[n_r(-d)], e_send.at[0, d], e_recv.at[0, d], row_peer(d)).wait_recv()

    for d in FAR_FIRST:
        e1(d).start()
    in1[r] = st[r]
    rows_t = lax.broadcasted_iota(jnp.int32, (TOK, TOK), 0)
    cols_s = lax.broadcasted_iota(jnp.int32, (TOK, TOK), 1)
    causal = rows_t >= cols_s

    def attend(h):
        q_h, g_h = qkv[:, head(h)], g_ref[:, head(h)]
        k_v, v_v = qkv[:, 512:640], qkv[:, 640:768]
        s = jnp.where(causal, nt(q_h, k_v), 0.0).astype(BF16)
        gsc = jnp.where(causal, nt(g_h, v_v), 0.0).astype(BF16)
        dq[:, head(h)] = nn(gsc, k_v)
        if h == 0:
            dk[...] = tn(gsc, q_h)
            dv[...] = tn(s, g_h)
        else:
            dk[...] += tn(gsc, q_h)
            dv[...] += tn(s, g_h)

    attend(0)
    pl.when(c == 0)(drain0)
    pl.when(c == 1)(drain1)
    for d in range(1, ROW):
        e1_wait(d)
    pieces = [in1[i].astype(F32) for i in range(ROW)]
    total = pieces[0]
    for i in range(1, ROW):
        total = total + pieces[i]
    tot[...] = total.astype(BF16)

    def e2(d):
        kind = jnp.where(y + d < NY, 0, 1)
        return copy(tot.at[kind], in2.at[y, kind], e_send.at[1, d], e_recv.at[1, d], {"y": n_y(d)})

    def e2_wait(d):
        kind = jnp.where(y - d >= 0, 0, 1)
        copy(tot.at[kind], in2.at[n_y(-d), kind], e_send.at[1, d], e_recv.at[1, d], {"y": n_y(d)}).wait_recv()

    for d in FAR_FIRST:
        e2(d).start()
    in2[y] = jnp.zeros_like(tot)
    attend(1)
    attend(2)
    for m in range(NY):
        sib_sent(m)
    for pair in [(d, k, s) for d in (0, 1) for k in range(1, HALF + 1) for s in range(SUBS)]:
        if z_has(*pair):
            z_msg(*pair).wait_send()
    for d in range(1, NY):
        e2_wait(d)
    before = jnp.zeros((HD // ROW, HD), F32)
    after = jnp.zeros((HD // ROW, HD), F32)
    for i in range(NY):
        one = in2[i, jnp.where(i < y, 0, 1)].astype(F32)
        before = before + jnp.where(i < y, one, 0.0)
        after = after + jnp.where(i > y, one, 0.0)
    for i in range(ROW):
        out3[i, 0] = before.astype(BF16)
        before = before + pieces[i][0]
    for i in reversed(range(ROW)):
        out3[i, 1] = after.astype(BF16)
        after = after + pieces[i][1]

    def e3(d):
        return copy(out3.at[n_r(d)], in3.at[r], e_send.at[2, d], e_recv.at[2, d], row_peer(d))

    def e3_wait(d):
        copy(out3.at[r], in3.at[n_r(-d)], e_send.at[2, d], e_recv.at[2, d], row_peer(d)).wait_recv()

    for d in FAR_FIRST:
        e3(d).start()
    in3[r] = out3[r]
    attend(3)
    for d in range(1, ROW):
        e3_wait(d)
    prefix = in3[:, 0].reshape(HD, HD)
    suffix = in3[:, 1].reshape(HD, HD)
    for h in range(GROUP):
        cross = nt(g_ref[:, head(h)], prefix)
        grads[:, head(h)] = (factor * (dq[:, head(h)] + cross)).astype(BF16)
    grads[:, 512:640] = (factor * dk[...] + nt(qkv[:, 640:768], suffix)).astype(BF16)
    grads[:, 640:768] = (factor * dv[...] + nn(qkv[:, 512:640], suffix)).astype(BF16)

    def share(dz, slot):
        part[slot] = nt(grads[...], wts[n_z(dz)].reshape(FEAT, WCOLS))

    def r_has(d, k, s):
        return k < HALF or (k == HALF and s in (R_PART if d == 0 else L_PART))

    def r_msg(d, k, s):
        ds = pl.ds(s * PIECE, PIECE)
        return copy(tx.at[d, k - 1, ds], rx.at[d, k - 1, ds], r_send.at[d, k, s], r_recv.at[d, k, s], zr if d == 0 else zl)

    def r_step(d, k, s):
        ds = pl.ds(s * PIECE, PIECE)
        value = part[d, ds]
        if r_has(d, k + 1, s):
            r_msg(d, k + 1, s).wait_recv()
            value = value + rx[d, k, ds].astype(F32)
        tx[d, k - 1, ds] = value.astype(BF16)
        r_msg(d, k, s).start()

    share(HALF, 0)
    for d in (0, 1):
        for s in (R_PART if d == 0 else L_PART):
            ds = pl.ds(s * PIECE, PIECE)
            tx[d, HALF - 1, ds] = part[0, ds].astype(BF16)
            r_msg(d, HALF, s).start()
    for d in range(1, ROW):
        e1(d).wait_send()
        e2(d).wait_send()
        e3(d).wait_send()
    for k in range(HALF - 1, 0, -1):
        share(k, 0)
        share(-k, 1)
        for i in range(PIECES):
            r_step(0, k, L_TURN[i])
            r_step(1, k, R_TURN[i])
    share(0, 0)
    for d in (0, 1):
        for k in range(2, HALF + 1):
            for s in range(PIECES):
                if r_has(d, k, s):
                    r_msg(d, k, s).wait_send()
    for i in range(PIECES):
        s = L_TURN[i]
        ds = pl.ds(s * PIECE, PIECE)
        r_msg(0, 1, s).wait_recv()
        r_msg(1, 1, s).wait_recv()
        total = part[0, ds] + rx[0, 0, ds].astype(F32) + rx[1, 0, ds].astype(F32)
        o_ref[ds] = total.astype(BF16)
    for d in (0, 1):
        for i in range(PIECES):
            r_msg(d, 1, i).wait_send()


def local(activations, grad_out, query_weight, key_weight, value_weight):
    dma = pltpu.SemaphoreType.DMA
    operands = (activations, grad_out, query_weight, key_weight, value_weight)
    operands = [pltpu.with_memory_space_constraint(v, pltpu.HBM) for v in operands]
    return pl.pallas_call(
        kernel,
        out_shape=jax.ShapeDtypeStruct((TOK, FEAT), BF16),
        in_specs=[pl.BlockSpec(memory_space=pltpu.HBM)] * 5,
        out_specs=pl.BlockSpec(memory_space=pltpu.VMEM),
        scratch_shapes=[
            pltpu.VMEM((NZ, TOK, FEAT), BF16),
            pltpu.VMEM((NY, NX, NC * WROWS, WCOLS), BF16),
            pltpu.VMEM((TOK, WCOLS), F32),
            pltpu.VMEM((TOK, WCOLS), BF16),
            pltpu.VMEM((TOK, FEAT), F32),
            pltpu.VMEM((TOK, HD), F32),
            pltpu.VMEM((TOK, HD), F32),
            pltpu.VMEM((TOK, WCOLS), BF16),
            pltpu.VMEM((4, TOK, FEAT), F32),
            pltpu.VMEM((2, HALF, TOK, FEAT), BF16),
            pltpu.VMEM((2, HALF, TOK, FEAT), BF16),
            pltpu.VMEM((ROW, 2, HD // ROW, HD), BF16),
            pltpu.VMEM((ROW, 2, HD // ROW, HD), BF16),
            pltpu.VMEM((2, HD // ROW, HD), BF16),
            pltpu.VMEM((NY, 2, HD // ROW, HD), BF16),
            pltpu.VMEM((ROW, 2, HD // ROW, HD), BF16),
            pltpu.VMEM((ROW, 2, HD // ROW, HD), BF16),
            pltpu.VMEM((TOK, FEAT), BF16),
            dma((5,)),
            dma((2, HALF + 1, SUBS)),
            dma((2, HALF + 1, SUBS)),
            dma((44,)),
            dma((44,)),
            dma((NY + 1,)),
            dma((NY + 1,)),
            dma((3, 8)),
            dma((3, 8)),
            dma((2, HALF + 1, PIECES)),
            dma((2, HALF + 1, PIECES)),
        ],
        compiler_params=pltpu.CompilerParams(
            collective_id=0, has_side_effects=True, vmem_limit_bytes=48 * 1024 * 1024
        ),
        cost_estimate=pl.CostEstimate(flops=4_000_000_000, bytes_accessed=2_000_000, transcendentals=0),
    )(*operands)


def solution(mesh):
    finer = Mesh(mesh.devices.reshape(NY, NX, NC, NZ), AXES)
    spec = P(SEQ, "head")
    return jax.shard_map(
        local, mesh=finer, in_specs=(spec,) * 5, out_specs=spec, check_vma=False
    )
```

```python
import jax
import jax.numpy as jnp
from jax import lax
from jax.experimental import pallas as pl
from jax.experimental.pallas import tpu as pltpu
from jax.sharding import Mesh
from jax.sharding import PartitionSpec as P

HEADS = 32
KV_HEADS = 8
HD = 128
GROUP = HEADS // KV_HEADS
NY, NX, NC, NZ = 8, 4, 2, 8
ROW = NX * NC
AXES = ("y", "x", "core", "head")
SEQ = ("y", "x", "core")
F32 = jnp.float32
BF16 = jnp.bfloat16
TOK = 256
FEAT = 512
WROWS = 64
WCOLS = 768
SUBS = 4
SUB = TOK // SUBS
HALF = NZ // 2
CUT = 64
REST = NC * WROWS - CUT


def halves(start, rows):
    first = (rows // 2 + 15) // 16 * 16
    return ((start, first), (start + first, rows - first))


CORE0 = (
    "near", (1, 0), 0, "far", 1, (1, 1), (1, 3), (2, 0), 2, 3, (1, 2), (2, 1), (2, 3), 4, (3, 0), 5,
    (2, 2), (3, 1), 6, (3, 3), 7, (4, 0), 8, (3, 2), 9, (4, 1), (4, 3), 10, (4, 2), 11,
)
CORE1 = (
    "y1", 0, "m0", 1, "y2", 2, "m-1", "m1", "e0", 3, "y3", 4, "e-1", "e1", "m-2", "m2", 5, 6,
    "y4", 7, "e-2", "e2", "m-3", "m3", 8, 9, "e-3", "e3", "m4", 10, 11, "e4",
)
PIECES = 2
PIECE = TOK // PIECES
R_TURN = tuple(range(PIECES))
R_PART, L_PART = R_TURN[: PIECES // 2], R_TURN[PIECES // 2 :]
L_TURN = L_PART + R_PART
FAR_FIRST = (4, 3, 5, 2, 6, 1, 7)
PARTS = (
    ((0, CUT),) + halves(0, CUT),
    ((CUT, REST),) + halves(CUT, REST),
)
R_ORDER = (0, 1, 2, 3)
L_ORDER = (2, 3, 0, 1)
R_LAST = (0, 1)
L_LAST = (2, 3)
X_ORDER = (0, 1, 3, 2)
XR_LAST = (0, 1)
XL_LAST = (3, 2)


def nt(a, b):
    return lax.dot_general(a, b, (((1,), (1,)), ((), ())), preferred_element_type=F32)


def tn(a, b):
    return lax.dot_general(a, b, (((0,), (0,)), ((), ())), preferred_element_type=F32)


def nn(a, b):
    return jnp.dot(a, b, preferred_element_type=F32)


def kernel(
    a_ref, go_ref, wq_ref, wk_ref, wv_ref, o_ref,
    act, wts, acc, qkv, dq, dk, dv, grads, part, tx, rx,
    st, in1, tot, in2, out3, in3,
    g_ref, i_sem, z_send, z_recv, w_send, w_recv, s_send, s_recv, e_send, e_recv, r_send, r_recv,
):
    y, x, c, z = (lax.axis_index(n) for n in AXES)
    r = x * NC + c
    n_y = lambda d: lax.rem(y + d + NY, NY)
    n_x = lambda d: lax.rem(x + d + NX, NX)
    n_z = lambda d: lax.rem(z + d + NZ, NZ)
    n_r = lambda d: lax.rem(r + d + ROW, ROW)
    zr, zl = {"head": n_z(1)}, {"head": n_z(-1)}
    yr, yl = {"y": n_y(1)}, {"y": n_y(-1)}
    xr, xl = {"x": n_x(1)}, {"x": n_x(-1)}
    sib = {"core": 1 - c}
    row_peer = lambda d: {"x": n_r(d) // NC, "core": lax.rem(n_r(d), NC)}

    own = pl.ds(pl.multiple_of(c * WROWS, WROWS), WROWS)
    loads = [
        pltpu.make_async_copy(a_ref, act.at[z], i_sem.at[0]),
        pltpu.make_async_copy(wq_ref, wts.at[y, x, own, pl.ds(0, 512)], i_sem.at[1]),
        pltpu.make_async_copy(wk_ref, wts.at[y, x, own, pl.ds(512, 128)], i_sem.at[2]),
        pltpu.make_async_copy(wv_ref, wts.at[y, x, own, pl.ds(640, 128)], i_sem.at[3]),
        pltpu.make_async_copy(go_ref, g_ref, i_sem.at[4]),
    ]
    for i in (1, 2, 3, 0, 4):
        loads[i].start()
    barrier = pltpu.get_barrier_semaphore()
    peers = [zr, zl, yr, yl, xr, xl, sib]
    for peer in peers:
        pl.semaphore_signal(barrier, inc=1, device_id=peer, device_id_type=pl.DeviceIdType.MESH)

    pl.semaphore_wait(barrier, len(peers))
    for load in loads[1:4]:
        load.wait()

    def copy(src, dst, ssem, rsem, dev):
        return pltpu.make_async_remote_copy(
            src_ref=src, dst_ref=dst, send_sem=ssem, recv_sem=rsem,
            device_id=dev, device_id_type=pl.DeviceIdType.MESH,
        )

    def same(ref, ssem, rsem, dev):
        return copy(ref, ref, ssem, rsem, dev)

    def z_msg(d, k, s):
        origin = n_z(1 - k) if d == 0 else n_z(k - 1)
        ref = act.at[origin, pl.ds(s * SUB, SUB)]
        if k == 1:
            return copy(
                a_ref.at[pl.ds(s * SUB, SUB)], ref, z_send.at[d, k, s], z_recv.at[d, k, s],
                zr if d == 0 else zl,
            )
        return same(ref, z_send.at[d, k, s], z_recv.at[d, k, s], zr if d == 0 else zl)

    def z_wait(d, k, s):
        origin = n_z(-k) if d == 0 else n_z(k)
        ref = act.at[origin, pl.ds(s * SUB, SUB)]
        same(ref, z_send.at[d, k, s], z_recv.at[d, k, s], zr if d == 0 else zl).wait_recv()

    def z_has(d, k, s):
        return k < HALF or (k == HALF and s in (R_LAST if d == 0 else L_LAST))

    def z_start():
        for i in range(SUBS):
            z_msg(0, 1, R_ORDER[i]).start()
            z_msg(1, 1, L_ORDER[i]).start()

    z_ticks = []
    for k in range(1, HALF + 1):
        for i in range(SUBS):
            pair = [(0, k, R_ORDER[i]), (1, k, L_ORDER[i])]
            pair = [p for p in pair if z_has(*p)]
            if pair:
                z_ticks.append(pair)

    def z_tick(i):
        for d, k, s in z_ticks[i]:
            z_wait(d, k, s)
            if z_has(d, k + 1, s):
                z_msg(d, k + 1, s).start()

    def w_ref(dy, dx, core, half=None):
        first, rows = PARTS[core][0 if half is None else 1 + half]
        return wts.at[n_y(dy), n_x(dx), pl.ds(first, rows)]

    def w_msg(ref, i, dev):
        return same(ref, w_send.at[i], w_recv.at[i], dev)

    def sib_ref(m, core):
        return wts.at[n_y(m), :, pl.ds(PARTS[core][0][0], PARTS[core][0][1])]

    def sib_msg(m, core):
        return same(sib_ref(m, core), s_send.at[m % NY], s_recv.at[m % NY], sib)

    def lend_msg():
        ref = wts.at[y, x, pl.ds(CUT, WROWS - CUT)]
        return same(ref, s_send.at[NY], s_recv.at[NY], sib)

    def make0():
        slot = lambda d, k, j: 4 + (d * 5 + k) * 4 + j

        def has(d, k, j):
            return k < 4 or (k == 4 and j in (XR_LAST if d == 0 else XL_LAST))

        def y_msg(d, k, j):
            dy = (1 - k) if d == 0 else (k - 1)
            return w_msg(w_ref(dy, j, 0), slot(d, k, j), yr if d == 0 else yl)

        def y_wait(d, k, j):
            dy = -k if d == 0 else k
            w_msg(w_ref(dy, j, 0), slot(d, k, j), yr if d == 0 else yl).wait_recv()

        def y_both(j):
            y_msg(0, 1, j).start()
            y_msg(1, 1, j).start()

        def x_near():
            w_msg(w_ref(0, 1, 0), 1, xl).wait_recv()
            w_msg(w_ref(0, 1, 0, 1), 3, xl).start()
            y_both(1)
            w_msg(w_ref(0, -1, 0), 0, xr).wait_recv()
            w_msg(w_ref(0, -1, 0, 0), 2, xr).start()
            y_both(3)

        def x_far():
            w_msg(w_ref(0, -2, 0, 0), 2, xr).wait_recv()
            w_msg(w_ref(0, 2, 0, 1), 3, xl).wait_recv()
            y_both(2)
            sib_msg(0, 0).start()

        def y_event(k, j):
            for d in (0, 1):
                if has(d, k, j):
                    y_wait(d, k, j)
                    if has(d, k + 1, j):
                        y_msg(d, k + 1, j).start()
            if j == 2:
                for m in (-k, k) if k < 4 else (4,):
                    sib_msg(m, 0).start()

        def run():
            if CUT < WROWS:
                lend_msg().start()
            w_msg(w_ref(0, 0, 0), 0, xr).start()
            w_msg(w_ref(0, 0, 0), 1, xl).start()
            y_both(0)
            z_start()
            for step in CORE0:
                if step == "near":
                    x_near()
                elif step == "far":
                    x_far()
                elif isinstance(step, int):
                    z_tick(step)
                else:
                    y_event(*step)

        def drain():
            if CUT < WROWS:
                lend_msg().wait_send()
            for i in range(4):
                dx, half, dev = ((0, None, xr), (0, None, xl), (-1, 0, xr), (1, 1, xl))[i]
                w_msg(w_ref(0, dx, 0, half), i, dev).wait_send()
            for k in range(1, 5):
                for j in range(4):
                    for d in (0, 1):
                        if has(d, k, j):
                            y_msg(d, k, j).wait_send()

        return run, drain

    def make1():
        def y_msg(d, k):
            dy = (1 - k) if d == 0 else (k - 1)
            half = None if k < 4 else d
            return w_msg(w_ref(dy, 0, 1, half), d * 5 + k, yr if d == 0 else yl)

        def y_wait(d, k):
            dy = -k if d == 0 else k
            half = None if k < 4 else d
            w_msg(w_ref(dy, 0, 1, half), d * 5 + k, yr if d == 0 else yl).wait_recv()

        def x_first(m):
            i = 10 + (m % NY) * 4
            return [w_msg(w_ref(m, 0, 1), i, xr), w_msg(w_ref(m, 0, 1), i + 1, xl)]

        def x_second(m, d):
            i = 10 + (m % NY) * 4
            return w_msg(w_ref(m, 2 * d - 1, 1, d), i + 2 + d, xl if d else xr)

        def x_send(m):
            for msg in x_first(m):
                msg.start()

        def x_mid(m):
            i = 10 + (m % NY) * 4
            w_msg(w_ref(m, -1, 1), i, xr).wait_recv()
            x_second(m, 0).start()
            w_msg(w_ref(m, 1, 1), i + 1, xl).wait_recv()
            x_second(m, 1).start()

        def x_end(m):
            i = 10 + (m % NY) * 4
            w_msg(w_ref(m, -2, 1, 0), i + 2, xr).wait_recv()
            w_msg(w_ref(m, 2, 1, 1), i + 3, xl).wait_recv()
            sib_msg(m, 1).start()

        def y_event(k):
            for d in (0, 1):
                y_wait(d, k)
                if k < 4:
                    y_msg(d, k + 1).start()
                    x_send(-k if d == 0 else k)
            if k == 4:
                x_send(4)

        def run():
            z_start()
            if CUT < WROWS:
                lend_msg().wait_recv()
            y_msg(0, 1).start()
            y_msg(1, 1).start()
            x_send(0)
            for step in CORE1:
                if isinstance(step, int):
                    z_tick(step)
                else:
                    (y_event, x_mid, x_end)["yme".index(step[0])](int(step[1:]))

        def drain():
            for d in (0, 1):
                for k in range(1, 5):
                    y_msg(d, k).wait_send()
            for m in range(NY):
                for msg in x_first(m) + [x_second(m, 0), x_second(m, 1)]:
                    msg.wait_send()

        return run, drain

    run0, drain0 = make0()
    run1, drain1 = make1()
    pl.when(c == 0)(run0)
    pl.when(c == 1)(run1)

    def sib_wait(m):
        def wait_for(core):
            same(sib_ref(m, core), s_send.at[m], s_recv.at[m], sib).wait_recv()

        pl.when(c == 0)(lambda: wait_for(1))
        pl.when(c == 1)(lambda: wait_for(0))

    def sib_sent(m):
        pl.when(c == 0)(lambda: sib_msg(m, 0).wait_send())
        pl.when(c == 1)(lambda: sib_msg(m, 1).wait_send())

    far_y, far_z = n_y(4), n_z(4)

    def project(f):
        acc[...] += nn(act[f], wts[f].reshape(FEAT, WCOLS))

    acc[...] = jnp.zeros_like(acc)
    loads[0].wait()
    loads[4].wait()
    for m in range(NY):
        if m != 4:
            sib_wait(m)

    @pl.loop(0, NZ)
    def _(f):
        @pl.when(jnp.logical_and(f != far_y, f != far_z))
        def _():
            project(f)

    sib_wait(4)

    @pl.when(far_y != far_z)
    def _():
        project(far_y)

    z_tick(12)
    z_tick(13)
    project(far_z)

    qkv[...] = acc[...].astype(BF16)
    head = lambda h: pl.ds(h * HD, HD)
    k_val, v_val = qkv[:, 512:640], qkv[:, 640:768]
    factor = HD ** -0.5
    kv = tn(k_val, v_val)
    gs = tn(qkv[:, head(0)], g_ref[:, head(0)])
    for h in range(1, GROUP):
        gs += tn(qkv[:, head(h)], g_ref[:, head(h)])
    st[:, 0] = kv.astype(BF16).reshape(ROW, HD // ROW, HD)
    st[:, 1] = (factor * gs).astype(BF16).reshape(ROW, HD // ROW, HD)

    def e1(d):
        return copy(st.at[n_r(d)], in1.at[r], e_send.at[0, d], e_recv.at[0, d], row_peer(d))

    def e1_wait(d):
        copy(st.at[r], in1.at[n_r(-d)], e_send.at[0, d], e_recv.at[0, d], row_peer(d)).wait_recv()

    for d in FAR_FIRST:
        e1(d).start()
    in1[r] = st[r]
    rows_t = lax.broadcasted_iota(jnp.int32, (TOK, TOK), 0)
    cols_s = lax.broadcasted_iota(jnp.int32, (TOK, TOK), 1)
    causal = rows_t >= cols_s

    def attend(h):
        q_h, g_h = qkv[:, head(h)], g_ref[:, head(h)]
        k_v, v_v = qkv[:, 512:640], qkv[:, 640:768]
        s = jnp.where(causal, nt(q_h, k_v), 0.0).astype(BF16)
        gsc = jnp.where(causal, nt(g_h, v_v), 0.0).astype(BF16)
        dq[:, head(h)] = nn(gsc, k_v)
        if h == 0:
            dk[...] = tn(gsc, q_h)
            dv[...] = tn(s, g_h)
        else:
            dk[...] += tn(gsc, q_h)
            dv[...] += tn(s, g_h)

    attend(0)
    pl.when(c == 0)(drain0)
    pl.when(c == 1)(drain1)
    for d in range(1, ROW):
        e1_wait(d)
    pieces = [in1[i].astype(F32) for i in range(ROW)]
    total = pieces[0]
    for i in range(1, ROW):
        total = total + pieces[i]
    tot[...] = total.astype(BF16)

    def e2(d):
        kind = jnp.where(y + d < NY, 0, 1)
        return copy(tot.at[kind], in2.at[y, kind], e_send.at[1, d], e_recv.at[1, d], {"y": n_y(d)})

    def e2_wait(d):
        kind = jnp.where(y - d >= 0, 0, 1)
        copy(tot.at[kind], in2.at[n_y(-d), kind], e_send.at[1, d], e_recv.at[1, d], {"y": n_y(d)}).wait_recv()

    for d in FAR_FIRST:
        e2(d).start()
    in2[y] = jnp.zeros_like(tot)
    attend(1)
    attend(2)
    for m in range(NY):
        sib_sent(m)
    for pair in [(d, k, s) for d in (0, 1) for k in range(1, HALF + 1) for s in range(SUBS)]:
        if z_has(*pair):
            z_msg(*pair).wait_send()
    for d in range(1, NY):
        e2_wait(d)
    before = jnp.zeros((HD // ROW, HD), F32)
    after = jnp.zeros((HD // ROW, HD), F32)
    for i in range(NY):
        one = in2[i, jnp.where(i < y, 0, 1)].astype(F32)
        before = before + jnp.where(i < y, one, 0.0)
        after = after + jnp.where(i > y, one, 0.0)
    for i in range(ROW):
        out3[i, 0] = before.astype(BF16)
        before = before + pieces[i][0]
    for i in reversed(range(ROW)):
        out3[i, 1] = after.astype(BF16)
        after = after + pieces[i][1]

    def e3(d):
        return copy(out3.at[n_r(d)], in3.at[r], e_send.at[2, d], e_recv.at[2, d], row_peer(d))

    def e3_wait(d):
        copy(out3.at[r], in3.at[n_r(-d)], e_send.at[2, d], e_recv.at[2, d], row_peer(d)).wait_recv()

    for d in FAR_FIRST:
        e3(d).start()
    in3[r] = out3[r]
    attend(3)
    for d in range(1, ROW):
        e3_wait(d)
    prefix = in3[:, 0].reshape(HD, HD)
    suffix = in3[:, 1].reshape(HD, HD)
    for h in range(GROUP):
        cross = nt(g_ref[:, head(h)], prefix)
        grads[:, head(h)] = (factor * (dq[:, head(h)] + cross)).astype(BF16)
    grads[:, 512:640] = (factor * dk[...] + nt(qkv[:, 640:768], suffix)).astype(BF16)
    grads[:, 640:768] = (factor * dv[...] + nn(qkv[:, 512:640], suffix)).astype(BF16)

    def share(dz, slot):
        part[slot] = nt(grads[...], wts[n_z(dz)].reshape(FEAT, WCOLS))

    def r_has(d, k, s):
        return k < HALF or (k == HALF and s in (R_PART if d == 0 else L_PART))

    def r_msg(d, k, s):
        ds = pl.ds(s * PIECE, PIECE)
        return copy(tx.at[d, k - 1, ds], rx.at[d, k - 1, ds], r_send.at[d, k, s], r_recv.at[d, k, s], zr if d == 0 else zl)

    def r_step(d, k, s):
        ds = pl.ds(s * PIECE, PIECE)
        value = part[d, ds]
        if r_has(d, k + 1, s):
            r_msg(d, k + 1, s).wait_recv()
            value = value + rx[d, k, ds].astype(F32)
        tx[d, k - 1, ds] = value.astype(BF16)
        r_msg(d, k, s).start()

    share(HALF, 0)
    for d in (0, 1):
        for s in (R_PART if d == 0 else L_PART):
            ds = pl.ds(s * PIECE, PIECE)
            tx[d, HALF - 1, ds] = part[0, ds].astype(BF16)
            r_msg(d, HALF, s).start()
    for d in range(1, ROW):
        e1(d).wait_send()
        e2(d).wait_send()
        e3(d).wait_send()
    for k in range(HALF - 1, 0, -1):
        share(k, 0)
        share(-k, 1)
        for i in range(PIECES):
            r_step(0, k, L_TURN[i])
            r_step(1, k, R_TURN[i])
    share(0, 0)
    for d in (0, 1):
        for k in range(2, HALF + 1):
            for s in range(PIECES):
                if r_has(d, k, s):
                    r_msg(d, k, s).wait_send()
    for i in range(PIECES):
        s = L_TURN[i]
        ds = pl.ds(s * PIECE, PIECE)
        r_msg(0, 1, s).wait_recv()
        r_msg(1, 1, s).wait_recv()
        total = part[0, ds] + rx[0, 0, ds].astype(F32) + rx[1, 0, ds].astype(F32)
        o_ref[ds] = total.astype(BF16)
    for d in (0, 1):
        for i in range(PIECES):
            r_msg(d, 1, i).wait_send()


def local(activations, grad_out, query_weight, key_weight, value_weight):
    dma = pltpu.SemaphoreType.DMA
    operands = (activations, grad_out, query_weight, key_weight, value_weight)
    operands = [pltpu.with_memory_space_constraint(v, pltpu.HBM) for v in operands]
    return pl.pallas_call(
        kernel,
        out_shape=jax.ShapeDtypeStruct((TOK, FEAT), BF16),
        in_specs=[pl.BlockSpec(memory_space=pltpu.HBM)] * 5,
        out_specs=pl.BlockSpec(memory_space=pltpu.VMEM),
        scratch_shapes=[
            pltpu.VMEM((NZ, TOK, FEAT), BF16),
            pltpu.VMEM((NY, NX, NC * WROWS, WCOLS), BF16),
            pltpu.VMEM((TOK, WCOLS), F32),
            pltpu.VMEM((TOK, WCOLS), BF16),
            pltpu.VMEM((TOK, FEAT), F32),
            pltpu.VMEM((TOK, HD), F32),
            pltpu.VMEM((TOK, HD), F32),
            pltpu.VMEM((TOK, WCOLS), BF16),
            pltpu.VMEM((4, TOK, FEAT), F32),
            pltpu.VMEM((2, HALF, TOK, FEAT), BF16),
            pltpu.VMEM((2, HALF, TOK, FEAT), BF16),
            pltpu.VMEM((ROW, 2, HD // ROW, HD), BF16),
            pltpu.VMEM((ROW, 2, HD // ROW, HD), BF16),
            pltpu.VMEM((2, HD // ROW, HD), BF16),
            pltpu.VMEM((NY, 2, HD // ROW, HD), BF16),
            pltpu.VMEM((ROW, 2, HD // ROW, HD), BF16),
            pltpu.VMEM((ROW, 2, HD // ROW, HD), BF16),
            pltpu.VMEM((TOK, FEAT), BF16),
            dma((5,)),
            dma((2, HALF + 1, SUBS)),
            dma((2, HALF + 1, SUBS)),
            dma((44,)),
            dma((44,)),
            dma((NY + 1,)),
            dma((NY + 1,)),
            dma((3, 8)),
            dma((3, 8)),
            dma((2, HALF + 1, PIECES)),
            dma((2, HALF + 1, PIECES)),
        ],
        compiler_params=pltpu.CompilerParams(
            collective_id=0, has_side_effects=True, vmem_limit_bytes=48 * 1024 * 1024
        ),
        cost_estimate=pl.CostEstimate(flops=4_000_000_000, bytes_accessed=2_000_000, transcendentals=0),
    )(*operands)


def solution(mesh):
    finer = Mesh(mesh.devices.reshape(NY, NX, NC, NZ), AXES)
    spec = P(SEQ, "head")
    return jax.shard_map(
        local, mesh=finer, in_specs=(spec,) * 5, out_specs=spec, check_vma=False
    )
```

```python
import jax
import jax.numpy as jnp
from jax import lax
from jax.experimental import pallas as pl
from jax.experimental.pallas import tpu as pltpu
from jax.sharding import Mesh
from jax.sharding import PartitionSpec as P

HEADS = 32
KV_HEADS = 8
HD = 128
GROUP = HEADS // KV_HEADS
NY, NX, NC, NZ = 8, 4, 2, 8
ROW = NX * NC
AXES = ("y", "x", "core", "head")
SEQ = ("y", "x", "core")
F32 = jnp.float32
BF16 = jnp.bfloat16
TOK = 256
FEAT = 512
WROWS = 64
WCOLS = 768
SUBS = 4
SUB = TOK // SUBS
HALF = NZ // 2
CUT = 64
REST = NC * WROWS - CUT


def halves(start, rows):
    first = (rows // 2 + 15) // 16 * 16
    return ((start, first), (start + first, rows - first))


CORE0 = (
    "near", (1, 0), 0, "far", 1, (1, 1), (1, 3), (2, 0), 2, 3, (1, 2), (2, 1), (2, 3), 4, (3, 0), 5,
    (2, 2), (3, 1), 6, (3, 3), 7, (4, 0), 8, (3, 2), 9, (4, 1), (4, 3), 10, (4, 2), 11,
)
CORE1 = (
    "y1", 0, "m0", 1, "y2", 2, "m-1", "m1", "e0", 3, "y3", 4, "e-1", "e1", "m-2", "m2", 5, 6,
    "y4", 7, "e-2", "e2", "m-3", "m3", 8, 9, "e-3", "e3", "m4", 10, 11, "e4",
)
PIECES = 2
PIECE = TOK // PIECES
R_TURN = tuple(range(PIECES))
R_PART, L_PART = R_TURN[: PIECES // 2], R_TURN[PIECES // 2 :]
L_TURN = L_PART + R_PART
FAR_FIRST = (4, 3, 5, 2, 6, 1, 7)
PARTS = (
    ((0, CUT),) + halves(0, CUT),
    ((CUT, REST),) + halves(CUT, REST),
)
R_ORDER = (0, 1, 2, 3)
L_ORDER = (2, 3, 0, 1)
R_LAST = (0, 1)
L_LAST = (2, 3)
X_ORDER = (0, 1, 3, 2)
XR_LAST = (0, 1)
XL_LAST = (3, 2)


def nt(a, b):
    return lax.dot_general(a, b, (((1,), (1,)), ((), ())), preferred_element_type=F32)


def tn(a, b):
    return lax.dot_general(a, b, (((0,), (0,)), ((), ())), preferred_element_type=F32)


def nn(a, b):
    return jnp.dot(a, b, preferred_element_type=F32)


def kernel(
    a_ref, go_ref, wq_ref, wk_ref, wv_ref, o_ref,
    act, wts, acc, qkv, dq, dk, dv, grads, part, tx, rx,
    st, in1, tot, in2, out3, in3,
    g_ref, i_sem, z_send, z_recv, w_send, w_recv, s_send, s_recv, e_send, e_recv, r_send, r_recv,
):
    y, x, c, z = (lax.axis_index(n) for n in AXES)
    r = x * NC + c
    n_y = lambda d: lax.rem(y + d + NY, NY)
    n_x = lambda d: lax.rem(x + d + NX, NX)
    n_z = lambda d: lax.rem(z + d + NZ, NZ)
    n_r = lambda d: lax.rem(r + d + ROW, ROW)
    zr, zl = {"head": n_z(1)}, {"head": n_z(-1)}
    yr, yl = {"y": n_y(1)}, {"y": n_y(-1)}
    xr, xl = {"x": n_x(1)}, {"x": n_x(-1)}
    sib = {"core": 1 - c}
    row_peer = lambda d: {"x": n_r(d) // NC, "core": lax.rem(n_r(d), NC)}

    barrier = pltpu.get_barrier_semaphore()
    peers = [zr, zl, yr, yl, xr, xl, sib]
    for peer in peers:
        pl.semaphore_signal(barrier, inc=1, device_id=peer, device_id_type=pl.DeviceIdType.MESH)

    own = pl.ds(pl.multiple_of(c * WROWS, WROWS), WROWS)
    loads = [
        pltpu.make_async_copy(a_ref, act.at[z], i_sem.at[0]),
        pltpu.make_async_copy(wq_ref, wts.at[y, x, own, pl.ds(0, 512)], i_sem.at[1]),
        pltpu.make_async_copy(wk_ref, wts.at[y, x, own, pl.ds(512, 128)], i_sem.at[2]),
        pltpu.make_async_copy(wv_ref, wts.at[y, x, own, pl.ds(640, 128)], i_sem.at[3]),
        pltpu.make_async_copy(go_ref, g_ref, i_sem.at[4]),
    ]
    for i in (1, 2, 3, 0, 4):
        loads[i].start()
    pl.semaphore_wait(barrier, len(peers))
    for load in loads[1:4]:
        load.wait()

    def copy(src, dst, ssem, rsem, dev):
        return pltpu.make_async_remote_copy(
            src_ref=src, dst_ref=dst, send_sem=ssem, recv_sem=rsem,
            device_id=dev, device_id_type=pl.DeviceIdType.MESH,
        )

    def same(ref, ssem, rsem, dev):
        return copy(ref, ref, ssem, rsem, dev)

    def z_msg(d, k, s):
        origin = n_z(1 - k) if d == 0 else n_z(k - 1)
        ref = act.at[origin, pl.ds(s * SUB, SUB)]
        if k == 1:
            return copy(
                a_ref.at[pl.ds(s * SUB, SUB)], ref, z_send.at[d, k, s], z_recv.at[d, k, s],
                zr if d == 0 else zl,
            )
        return same(ref, z_send.at[d, k, s], z_recv.at[d, k, s], zr if d == 0 else zl)

    def z_wait(d, k, s):
        origin = n_z(-k) if d == 0 else n_z(k)
        ref = act.at[origin, pl.ds(s * SUB, SUB)]
        same(ref, z_send.at[d, k, s], z_recv.at[d, k, s], zr if d == 0 else zl).wait_recv()

    def z_has(d, k, s):
        return k < HALF or (k == HALF and s in (R_LAST if d == 0 else L_LAST))

    def z_start():
        for i in range(SUBS):
            z_msg(0, 1, R_ORDER[i]).start()
            z_msg(1, 1, L_ORDER[i]).start()

    z_ticks = []
    for k in range(1, HALF + 1):
        for i in range(SUBS):
            pair = [(0, k, R_ORDER[i]), (1, k, L_ORDER[i])]
            pair = [p for p in pair if z_has(*p)]
            if pair:
                z_ticks.append(pair)

    def z_tick(i):
        for d, k, s in z_ticks[i]:
            z_wait(d, k, s)
            if z_has(d, k + 1, s):
                z_msg(d, k + 1, s).start()

    def w_ref(dy, dx, core, half=None):
        first, rows = PARTS[core][0 if half is None else 1 + half]
        return wts.at[n_y(dy), n_x(dx), pl.ds(first, rows)]

    def w_msg(ref, i, dev):
        return same(ref, w_send.at[i], w_recv.at[i], dev)

    def sib_ref(m, core):
        return wts.at[n_y(m), :, pl.ds(PARTS[core][0][0], PARTS[core][0][1])]

    def sib_msg(m, core):
        return same(sib_ref(m, core), s_send.at[m % NY], s_recv.at[m % NY], sib)

    def lend_msg():
        ref = wts.at[y, x, pl.ds(CUT, WROWS - CUT)]
        return same(ref, s_send.at[NY], s_recv.at[NY], sib)

    def make0():
        slot = lambda d, k, j: 4 + (d * 5 + k) * 4 + j

        def has(d, k, j):
            return k < 4 or (k == 4 and j in (XR_LAST if d == 0 else XL_LAST))

        def y_msg(d, k, j):
            dy = (1 - k) if d == 0 else (k - 1)
            return w_msg(w_ref(dy, j, 0), slot(d, k, j), yr if d == 0 else yl)

        def y_wait(d, k, j):
            dy = -k if d == 0 else k
            w_msg(w_ref(dy, j, 0), slot(d, k, j), yr if d == 0 else yl).wait_recv()

        def y_both(j):
            y_msg(0, 1, j).start()
            y_msg(1, 1, j).start()

        def x_near():
            w_msg(w_ref(0, 1, 0), 1, xl).wait_recv()
            w_msg(w_ref(0, 1, 0, 1), 3, xl).start()
            y_both(1)
            w_msg(w_ref(0, -1, 0), 0, xr).wait_recv()
            w_msg(w_ref(0, -1, 0, 0), 2, xr).start()
            y_both(3)

        def x_far():
            w_msg(w_ref(0, -2, 0, 0), 2, xr).wait_recv()
            w_msg(w_ref(0, 2, 0, 1), 3, xl).wait_recv()
            y_both(2)
            sib_msg(0, 0).start()

        def y_event(k, j):
            for d in (0, 1):
                if has(d, k, j):
                    y_wait(d, k, j)
                    if has(d, k + 1, j):
                        y_msg(d, k + 1, j).start()
            if j == 2:
                for m in (-k, k) if k < 4 else (4,):
                    sib_msg(m, 0).start()

        def run():
            if CUT < WROWS:
                lend_msg().start()
            w_msg(w_ref(0, 0, 0), 0, xr).start()
            w_msg(w_ref(0, 0, 0), 1, xl).start()
            y_both(0)
            z_start()
            for step in CORE0:
                if step == "near":
                    x_near()
                elif step == "far":
                    x_far()
                elif isinstance(step, int):
                    z_tick(step)
                else:
                    y_event(*step)

        def drain():
            if CUT < WROWS:
                lend_msg().wait_send()
            for i in range(4):
                dx, half, dev = ((0, None, xr), (0, None, xl), (-1, 0, xr), (1, 1, xl))[i]
                w_msg(w_ref(0, dx, 0, half), i, dev).wait_send()
            for k in range(1, 5):
                for j in range(4):
                    for d in (0, 1):
                        if has(d, k, j):
                            y_msg(d, k, j).wait_send()

        return run, drain

    def make1():
        def y_msg(d, k):
            dy = (1 - k) if d == 0 else (k - 1)
            half = None if k < 4 else d
            return w_msg(w_ref(dy, 0, 1, half), d * 5 + k, yr if d == 0 else yl)

        def y_wait(d, k):
            dy = -k if d == 0 else k
            half = None if k < 4 else d
            w_msg(w_ref(dy, 0, 1, half), d * 5 + k, yr if d == 0 else yl).wait_recv()

        def x_first(m):
            i = 10 + (m % NY) * 4
            return [w_msg(w_ref(m, 0, 1), i, xr), w_msg(w_ref(m, 0, 1), i + 1, xl)]

        def x_second(m, d):
            i = 10 + (m % NY) * 4
            return w_msg(w_ref(m, 2 * d - 1, 1, d), i + 2 + d, xl if d else xr)

        def x_send(m):
            for msg in x_first(m):
                msg.start()

        def x_mid(m):
            i = 10 + (m % NY) * 4
            w_msg(w_ref(m, -1, 1), i, xr).wait_recv()
            x_second(m, 0).start()
            w_msg(w_ref(m, 1, 1), i + 1, xl).wait_recv()
            x_second(m, 1).start()

        def x_end(m):
            i = 10 + (m % NY) * 4
            w_msg(w_ref(m, -2, 1, 0), i + 2, xr).wait_recv()
            w_msg(w_ref(m, 2, 1, 1), i + 3, xl).wait_recv()
            sib_msg(m, 1).start()

        def y_event(k):
            for d in (0, 1):
                y_wait(d, k)
                if k < 4:
                    y_msg(d, k + 1).start()
                    x_send(-k if d == 0 else k)
            if k == 4:
                x_send(4)

        def run():
            z_start()
            if CUT < WROWS:
                lend_msg().wait_recv()
            y_msg(0, 1).start()
            y_msg(1, 1).start()
            x_send(0)
            for step in CORE1:
                if isinstance(step, int):
                    z_tick(step)
                else:
                    (y_event, x_mid, x_end)["yme".index(step[0])](int(step[1:]))

        def drain():
            for d in (0, 1):
                for k in range(1, 5):
                    y_msg(d, k).wait_send()
            for m in range(NY):
                for msg in x_first(m) + [x_second(m, 0), x_second(m, 1)]:
                    msg.wait_send()

        return run, drain

    run0, drain0 = make0()
    run1, drain1 = make1()
    pl.when(c == 0)(run0)
    pl.when(c == 1)(run1)

    def sib_wait(m):
        def wait_for(core):
            same(sib_ref(m, core), s_send.at[m], s_recv.at[m], sib).wait_recv()

        pl.when(c == 0)(lambda: wait_for(1))
        pl.when(c == 1)(lambda: wait_for(0))

    def sib_sent(m):
        pl.when(c == 0)(lambda: sib_msg(m, 0).wait_send())
        pl.when(c == 1)(lambda: sib_msg(m, 1).wait_send())

    far_y, far_z = n_y(4), n_z(4)

    def project(f):
        acc[...] += nn(act[f], wts[f].reshape(FEAT, WCOLS))

    acc[...] = jnp.zeros_like(acc)
    loads[0].wait()
    loads[4].wait()
    for m in range(NY):
        if m != 4:
            sib_wait(m)

    @pl.loop(0, NZ)
    def _(f):
        @pl.when(jnp.logical_and(f != far_y, f != far_z))
        def _():
            project(f)

    sib_wait(4)

    @pl.when(far_y != far_z)
    def _():
        project(far_y)

    z_tick(12)
    z_tick(13)
    project(far_z)

    qkv[...] = acc[...].astype(BF16)
    head = lambda h: pl.ds(h * HD, HD)
    k_val, v_val = qkv[:, 512:640], qkv[:, 640:768]
    factor = HD ** -0.5
    kv = tn(k_val, v_val)
    gs = tn(qkv[:, head(0)], g_ref[:, head(0)])
    for h in range(1, GROUP):
        gs += tn(qkv[:, head(h)], g_ref[:, head(h)])
    st[:, 0] = kv.astype(BF16).reshape(ROW, HD // ROW, HD)
    st[:, 1] = (factor * gs).astype(BF16).reshape(ROW, HD // ROW, HD)

    def e1(d):
        return copy(st.at[n_r(d)], in1.at[r], e_send.at[0, d], e_recv.at[0, d], row_peer(d))

    def e1_wait(d):
        copy(st.at[r], in1.at[n_r(-d)], e_send.at[0, d], e_recv.at[0, d], row_peer(d)).wait_recv()

    for d in FAR_FIRST:
        e1(d).start()
    in1[r] = st[r]
    rows_t = lax.broadcasted_iota(jnp.int32, (TOK, TOK), 0)
    cols_s = lax.broadcasted_iota(jnp.int32, (TOK, TOK), 1)
    causal = rows_t >= cols_s

    def attend(h):
        q_h, g_h = qkv[:, head(h)], g_ref[:, head(h)]
        k_v, v_v = qkv[:, 512:640], qkv[:, 640:768]
        s = jnp.where(causal, nt(q_h, k_v), 0.0).astype(BF16)
        gsc = jnp.where(causal, nt(g_h, v_v), 0.0).astype(BF16)
        dq[:, head(h)] = nn(gsc, k_v)
        if h == 0:
            dk[...] = tn(gsc, q_h)
            dv[...] = tn(s, g_h)
        else:
            dk[...] += tn(gsc, q_h)
            dv[...] += tn(s, g_h)

    attend(0)
    pl.when(c == 0)(drain0)
    pl.when(c == 1)(drain1)
    for d in range(1, ROW):
        e1_wait(d)
    pieces = [in1[i].astype(F32) for i in range(ROW)]
    total = pieces[0]
    for i in range(1, ROW):
        total = total + pieces[i]
    tot[...] = total.astype(BF16)

    def e2(d):
        kind = jnp.where(y + d < NY, 0, 1)
        return copy(tot.at[kind], in2.at[y, kind], e_send.at[1, d], e_recv.at[1, d], {"y": n_y(d)})

    def e2_wait(d):
        kind = jnp.where(y - d >= 0, 0, 1)
        copy(tot.at[kind], in2.at[n_y(-d), kind], e_send.at[1, d], e_recv.at[1, d], {"y": n_y(d)}).wait_recv()

    for d in FAR_FIRST:
        e2(d).start()
    in2[y] = jnp.zeros_like(tot)
    attend(1)
    attend(2)
    for m in range(NY):
        sib_sent(m)
    for pair in [(d, k, s) for d in (0, 1) for k in range(1, HALF + 1) for s in range(SUBS)]:
        if z_has(*pair):
            z_msg(*pair).wait_send()
    for d in range(1, NY):
        e2_wait(d)
    before = jnp.zeros((HD // ROW, HD), F32)
    after = jnp.zeros((HD // ROW, HD), F32)
    for i in range(NY):
        one = in2[i, jnp.where(i < y, 0, 1)].astype(F32)
        before = before + jnp.where(i < y, one, 0.0)
        after = after + jnp.where(i > y, one, 0.0)
    for i in range(ROW):
        out3[i, 0] = before.astype(BF16)
        before = before + pieces[i][0]
    for i in reversed(range(ROW)):
        out3[i, 1] = after.astype(BF16)
        after = after + pieces[i][1]

    def e3(d):
        return copy(out3.at[n_r(d)], in3.at[r], e_send.at[2, d], e_recv.at[2, d], row_peer(d))

    def e3_wait(d):
        copy(out3.at[r], in3.at[n_r(-d)], e_send.at[2, d], e_recv.at[2, d], row_peer(d)).wait_recv()

    for d in FAR_FIRST:
        e3(d).start()
    in3[r] = out3[r]
    attend(3)
    for d in range(1, ROW):
        e3_wait(d)
    prefix = in3[:, 0].reshape(HD, HD)
    suffix = in3[:, 1].reshape(HD, HD)
    for h in range(GROUP):
        cross = nt(g_ref[:, head(h)], prefix)
        grads[:, head(h)] = (factor * (dq[:, head(h)] + cross)).astype(BF16)
    grads[:, 512:640] = (factor * dk[...] + nt(qkv[:, 640:768], suffix)).astype(BF16)
    grads[:, 640:768] = (factor * dv[...] + nn(qkv[:, 512:640], suffix)).astype(BF16)

    def share(dz, slot):
        part[slot] = nt(grads[...], wts[n_z(dz)].reshape(FEAT, WCOLS))

    def r_has(d, k, s):
        return k < HALF or (k == HALF and s in (R_PART if d == 0 else L_PART))

    def r_msg(d, k, s):
        ds = pl.ds(s * PIECE, PIECE)
        return copy(tx.at[d, k - 1, ds], rx.at[d, k - 1, ds], r_send.at[d, k, s], r_recv.at[d, k, s], zr if d == 0 else zl)

    def r_step(d, k, s):
        ds = pl.ds(s * PIECE, PIECE)
        value = part[d, ds]
        if r_has(d, k + 1, s):
            r_msg(d, k + 1, s).wait_recv()
            value = value + rx[d, k, ds].astype(F32)
        tx[d, k - 1, ds] = value.astype(BF16)
        r_msg(d, k, s).start()

    share(HALF, 0)
    for d in (0, 1):
        for s in (R_PART if d == 0 else L_PART):
            ds = pl.ds(s * PIECE, PIECE)
            tx[d, HALF - 1, ds] = part[0, ds].astype(BF16)
            r_msg(d, HALF, s).start()
    for d in range(1, ROW):
        e1(d).wait_send()
        e2(d).wait_send()
        e3(d).wait_send()
    for k in range(HALF - 1, 0, -1):
        share(k, 0)
        share(-k, 1)
        for i in range(PIECES):
            r_step(0, k, L_TURN[i])
            r_step(1, k, R_TURN[i])
    share(0, 0)
    for d in (0, 1):
        for k in range(2, HALF + 1):
            for s in range(PIECES):
                if r_has(d, k, s):
                    r_msg(d, k, s).wait_send()
    for i in range(PIECES):
        s = L_TURN[i]
        ds = pl.ds(s * PIECE, PIECE)
        r_msg(0, 1, s).wait_recv()
        r_msg(1, 1, s).wait_recv()
        total = part[0, ds] + rx[0, 0, ds].astype(F32) + rx[1, 0, ds].astype(F32)
        o_ref[ds] = total.astype(BF16)
    for d in (0, 1):
        for i in range(PIECES):
            r_msg(d, 1, i).wait_send()


def local(activations, grad_out, query_weight, key_weight, value_weight):
    dma = pltpu.SemaphoreType.DMA
    operands = (activations, grad_out, query_weight, key_weight, value_weight)
    operands = [pltpu.with_memory_space_constraint(v, pltpu.HBM) for v in operands]
    return pl.pallas_call(
        kernel,
        out_shape=jax.ShapeDtypeStruct((TOK, FEAT), BF16),
        in_specs=[pl.BlockSpec(memory_space=pltpu.HBM)] * 5,
        out_specs=pl.BlockSpec(memory_space=pltpu.VMEM),
        scratch_shapes=[
            pltpu.VMEM((NZ, TOK, FEAT), BF16),
            pltpu.VMEM((NY, NX, NC * WROWS, WCOLS), BF16),
            pltpu.VMEM((TOK, WCOLS), F32),
            pltpu.VMEM((TOK, WCOLS), BF16),
            pltpu.VMEM((TOK, FEAT), F32),
            pltpu.VMEM((TOK, HD), F32),
            pltpu.VMEM((TOK, HD), F32),
            pltpu.VMEM((TOK, WCOLS), BF16),
            pltpu.VMEM((4, TOK, FEAT), F32),
            pltpu.VMEM((2, HALF, TOK, FEAT), BF16),
            pltpu.VMEM((2, HALF, TOK, FEAT), BF16),
            pltpu.VMEM((ROW, 2, HD // ROW, HD), BF16),
            pltpu.VMEM((ROW, 2, HD // ROW, HD), BF16),
            pltpu.VMEM((2, HD // ROW, HD), BF16),
            pltpu.VMEM((NY, 2, HD // ROW, HD), BF16),
            pltpu.VMEM((ROW, 2, HD // ROW, HD), BF16),
            pltpu.VMEM((ROW, 2, HD // ROW, HD), BF16),
            pltpu.VMEM((TOK, FEAT), BF16),
            dma((5,)),
            dma((2, HALF + 1, SUBS)),
            dma((2, HALF + 1, SUBS)),
            dma((44,)),
            dma((44,)),
            dma((NY + 1,)),
            dma((NY + 1,)),
            dma((3, 8)),
            dma((3, 8)),
            dma((2, HALF + 1, PIECES)),
            dma((2, HALF + 1, PIECES)),
        ],
        compiler_params=pltpu.CompilerParams(
            collective_id=0, has_side_effects=True, vmem_limit_bytes=48 * 1024 * 1024
        ),
        cost_estimate=pl.CostEstimate(flops=4_000_000_000, bytes_accessed=2_000_000, transcendentals=0),
    )(*operands)


def solution(mesh):
    finer = Mesh(mesh.devices.reshape(NY, NX, NC, NZ), AXES)
    spec = P(SEQ, "head")
    return jax.shard_map(
        local, mesh=finer, in_specs=(spec,) * 5, out_specs=spec, check_vma=False
    )
```
